32 devices in a mesh: pb: 4 (over y, core), pa: 8 (over z, x).
Axes of the slice: x: 2, y: 2, z: 4, core: 2. Of those that a mesh axis runs over, the one named last changes fastest.
Arguments:
- questions: bfloat16 [256, 64, 768], P(('pb', 'pa')), may hold values from -6 to 6
- passages: bfloat16 [128, 256, 768], P(('pb', 'pa')), may hold values from -6 to 6
- cot_questions: bfloat16 [256, 64, 768], P(('pb', 'pa')), may hold values from -2.390625 to 2.390625
- cot_passages: bfloat16 [128, 256, 768], P(('pb', 'pa')), may hold values from -2.390625 to 2.390625
- question_lengths: int32 [256], P(('pb', 'pa')), may hold values from 16 to 64
- segment_lengths: int32 [128, 4], P(('pb', 'pa')), may hold values from 1 to 128, 256 in all within a row
- positives: int32 [256], P('pb'), may hold values from 0 to 511
- w_qkv: bfloat16 [2, 768, 2304], P(None, 'pb', 'pa'), may hold values from -0.21875 to 0.21875
- w_out: bfloat16 [2, 768, 768], P(None, 'pb', 'pa'), may hold values from -1.25 to 1.25
- w_up: bfloat16 [2, 768, 3072], P(None, 'pb', 'pa'), may hold values from -0.21875 to 0.21875
- w_down: bfloat16 [2, 3072, 768], P(None, 'pb', 'pa'), may hold values from -0.109375 to 0.109375
- norm_bias: bfloat16 [2, 8, 768], P(None, 'pb', 'pa'), may hold values from -0.59765625 to 1.4453125, as said below
- bias_up: bfloat16 [2, 3072], P(None, ('pb', 'pa')), may hold values from -1.1953125 to 1.1953125
Outputs:
- question_encodings: bfloat16 [256, 64, 768], P(('pb', 'pa'))
- passage_encodings: bfloat16 [128, 256, 768], P(('pb', 'pa'))
- question_losses: float32 [256], P(('pb', 'pa'))
- grad_questions: float32 [256, 64, 768], P(('pb', 'pa'))
- grad_passages: float32 [128, 256, 768], P(('pb', 'pa'))
- grad_w_qkv: float32 [2, 768, 2304], P(None, 'pb', 'pa')
- grad_w_out: float32 [2, 768, 768], P(None, 'pb', 'pa')
- grad_w_up: float32 [2, 768, 3072], P(None, 'pb', 'pa')
- grad_w_down: float32 [2, 3072, 768], P(None, 'pb', 'pa')
- grad_norm_bias: float32 [2, 8, 768], P(None, 'pb', 'pa')
- grad_bias_up: float32 [2, 3072], P(None, ('pb', 'pa'))
The draws below stay inside these ranges and needn't reach their ends.
Inputs may be any that keep to these rules, and one draw needn't show every extreme that they name: `segment_lengths`: the 4 lengths of every row sum to 256. `norm_bias`: per encoder, rows 0 and 2 are norm gains near one, the other rows shifts and biases.
All inputs are finite; a program needn't handle non-finite values.
Results may differ from the reference program's by a relative error of at most 0.019.
Values may be sent and summed in bfloat16 or wider, within the bound.
No kernel may reach another device: no remote copies, remote signals or barrier semaphores. Data moves between devices by JAX's collectives and lax.ppermute only.
A program may use at most 320 MiB of HBM per device.

```python
import math
import jax
import jax.numpy as jnp
import numpy as np
from jax import lax

D = 768
HD = 64
FF = 3072
LQ = 64
LP = 256
SEGS = 4
NQ = 256
NR = 128
NP = 512


def draw_norm_bias(key, part):
    key = jax.random.fold_in(key, 7)
    gain_key, shift_key = jax.random.split(key)
    gain_rows = jnp.clip(1.0 + 0.15 * jax.random.normal(gain_key, (2, 2, D), jnp.float32), 0.5546875, 1.4453125)
    shift_rows = jnp.clip(0.2 * jax.random.normal(shift_key, (2, 6, D), jnp.float32), -0.59765625, 0.59765625)
    stacked = jnp.stack([gain_rows[:, 0], shift_rows[:, 0], gain_rows[:, 1], shift_rows[:, 1], shift_rows[:, 2], shift_rows[:, 3], shift_rows[:, 4], shift_rows[:, 5]], axis=1)
    return stacked.astype(jnp.bfloat16)


def touch_ends(result, rng, least, high):
    longest = result.shape.index(max(result.shape))
    spots = []
    for shift in (0, 1):
        where = [jax.random.randint(jax.random.fold_in(rng, axis), (), 0, length) for axis, length in enumerate(result.shape)]
        where[longest] = (where[longest] + shift) % result.shape[longest]
        spots.append(tuple(where))
    return result.at[spots[0]].set(least).at[spots[1]].set(high)


def block_scale(stream_key, dims, pieces, smallest, top_value):
    loudness, own = 1.0, jax.random.fold_in(stream_key, 6)
    for dim, blocks in pieces:
        steps = jnp.exp(jax.random.uniform(jax.random.fold_in(own, dim), (blocks,), jnp.float32, smallest / len(pieces), top_value / len(pieces)))
        loudness = loudness * jnp.repeat(steps, dims[dim] // blocks).reshape([-1 if axis == dim else 1 for axis in range(len(dims))])
    return loudness


def length_profile(number_of, total, most, lean):
    loads = [(1 << 20) // math.isqrt(standing ** lean) + 1 for standing in range(2, number_of + 1)]
    spare, counts = total - most - (number_of - 1), [1] * (number_of - 1)
    while spare > 0:
        movable = [i for i in range(number_of - 1) if counts[i] < most]
        mass, budget = sum([loads[i] for i in movable]), spare
        for i in movable:
            extra = min(most - counts[i], max(1, budget * loads[i] // mass), spare)
            counts[i] = counts[i] + extra
            spare = spare - extra
    return np.array([most] + counts)


def uneven(stream_key, number_of, total, most, lean):
    if number_of == 2:
        one = jax.random.randint(stream_key, (), max(1, total - most), min(most, total - 1) + 1)
        return jnp.stack([one, total - one])
    sizes = jnp.asarray(length_profile(number_of, total, most, lean), jnp.int32)
    pairs = (number_of - 1) // 2
    donor, receiver = sizes[1:1 + 2 * pairs:2], sizes[2:2 + 2 * pairs:2]
    room = jnp.minimum(donor - 1, most - receiver)
    shifted = jax.random.randint(jax.random.fold_in(stream_key, 1), (pairs,), 0, 1 << 20) % (room + 1)
    sizes = sizes.at[1:1 + 2 * pairs:2].set(donor - shifted).at[2:2 + 2 * pairs:2].set(receiver + shifted)
    return sizes[jax.random.permutation(jax.random.fold_in(stream_key, 2), number_of)]


def noise(rng, dims, deviation, most, shards=(), kind=jnp.bfloat16):
    values = deviation * jax.random.normal(rng, dims, jnp.float32)
    if shards:
        values = values * block_scale(rng, dims, shards, -0.22, 0.18)
    return jnp.clip(values, -most, most).astype(kind)


def setup_inputs(seed: int = 0) -> dict:
    keys = jax.random.split(jax.random.key(seed), 14)
    questions = noise(keys[0], (NQ, LQ, D), 1.0, 6.0, ((0, 32),))
    passages = noise(keys[1], (NR, LP, D), 1.0, 6.0, ((0, 32),))
    cot_questions = noise(keys[2], (NQ, LQ, D), 0.4, 2.390625, ((0, 32),))
    cot_passages = noise(keys[3], (NR, LP, D), 0.4, 2.390625, ((0, 32),))
    question_lengths = touch_ends(jax.random.randint(keys[4], (NQ,), LQ // 4, LQ + 1), jax.random.fold_in(keys[4], 1), LQ // 4, LQ).astype(jnp.int32)
    segment_lengths = jax.vmap(lambda own: uneven(own, SEGS, LP, LP // 2, 2))(jax.random.split(keys[5], NR)).reshape((NR, SEGS)).astype(jnp.int32)
    positives = touch_ends(jax.random.randint(keys[6], (NQ,), 0, NP), jax.random.fold_in(keys[6], 1), 0, NP - 1).astype(jnp.int32)
    w_qkv = noise(keys[7], (2, D, 3 * D), D ** -0.5, 0.21875, ((1, 4), (2, 8)))
    w_out = noise(keys[8], (2, D, D), (D // 32) ** -0.5, 1.25, ((1, 4), (2, 8)))
    w_up = noise(keys[9], (2, D, FF), D ** -0.5, 0.21875, ((1, 4), (2, 8)))
    w_down = noise(keys[10], (2, FF, D), FF ** -0.5, 0.109375, ((1, 4), (2, 8)))
    norm_bias = draw_norm_bias(jax.random.fold_in(keys[13], 71), 0)
    bias_up = noise(keys[12], (2, FF), 0.2, 1.1953125, ((1, 32),))
    return dict(questions=questions, passages=passages, cot_questions=cot_questions, cot_passages=cot_passages, question_lengths=question_lengths, segment_lengths=segment_lengths, positives=positives, w_qkv=w_qkv, w_out=w_out, w_up=w_up, w_down=w_down, norm_bias=norm_bias, bias_up=bias_up)


NEG_FILL = -1000000000.0
EPSILON = 1e-06
ROOT_HALF = 0.7071067811865476

@jax.custom_vjp
def low(v):
    return lax.optimization_barrier(v.astype(jnp.bfloat16)).astype(jnp.float32)

@jax.custom_vjp
def low_back(v):
    return v

def low_keep(v):
    return (low(v), None)

def low_pass(kept, grad):
    return (grad,)

def back_keep(v):
    return (v, None)

def back_low(kept, grad):
    return (low(grad),)
low.defvjp(low_keep, low_pass)
low_back.defvjp(back_keep, back_low)

def matmul_high(left_side, right_side):
    return jnp.matmul(left_side, right_side, precision=lax.Precision.HIGHEST)

def rounded_both(tensor):
    return low(low_back(tensor))

def gelu_value(pre_act):
    return 0.5 * pre_act * (1.0 + lax.erf(pre_act * ROOT_HALF))

def norm_rows(summed, gain_vec, shift_vec):
    row_mean = lax.optimization_barrier(jnp.mean(summed, axis=-1, keepdims=True))
    centred = summed - row_mean
    inverse = lax.rsqrt(lax.optimization_barrier(jnp.mean(centred * centred, axis=-1, keepdims=True)) + EPSILON)
    return centred * inverse * gain_vec + shift_vec

def encoder_layer(inputs, allowed, weights):
    w_qkv, w_out, w_up, w_down, vectors, bias_up = weights
    seq_count, seq_len, model_dim = inputs.shape
    head_count = model_dim // HD
    head_shape = (seq_count, seq_len, head_count, HD)
    projected = matmul_high(inputs, w_qkv)
    queries = rounded_both(projected[..., :model_dim] + vectors[4]).reshape(head_shape)
    key_rows = rounded_both(projected[..., model_dim:2 * model_dim]).reshape(head_shape)
    values = rounded_both(projected[..., 2 * model_dim:] + vectors[5]).reshape(head_shape)
    raw_scores = low_back(jnp.einsum('bqhd,bkhd->bhqk', queries, key_rows, precision=lax.Precision.HIGHEST) * HD ** (-0.5))
    scores = jnp.where(allowed[:, None], raw_scores, NEG_FILL)
    row_peak = lax.optimization_barrier(jnp.max(scores, axis=-1, keepdims=True))
    exp_terms = jnp.exp(scores - row_peak)
    prob_low = low(exp_terms / lax.optimization_barrier(jnp.sum(exp_terms, axis=-1, keepdims=True)))
    attended = rounded_both(jnp.einsum('bhqk,bkhd->bqhd', prob_low, values, precision=lax.Precision.HIGHEST).reshape(seq_count, seq_len, model_dim))
    branch = low_back(matmul_high(attended, w_out) + vectors[6])
    first_norm = norm_rows(inputs + branch, vectors[0], vectors[1])
    hidden = low_back(matmul_high(low(first_norm), w_up) + bias_up)
    down_part = low_back(matmul_high(low(gelu_value(hidden)), w_down) + vectors[7])
    return norm_rows(first_norm + down_part, vectors[2], vectors[3])

def encode_groups(inputs, allowed, weights, group_size):
    group_count = inputs.shape[0] // group_size
    stacked_in = inputs.reshape((group_count, group_size) + inputs.shape[1:])
    stacked_mask = allowed.reshape((group_count, group_size) + allowed.shape[1:])
    step_fn = jax.checkpoint(lambda operands: encoder_layer(operands[0], operands[1], weights))
    return lax.map(step_fn, (stacked_in, stacked_mask)).reshape(inputs.shape)

def reference(questions, passages, cot_questions, cot_passages, question_lengths, segment_lengths, positives, w_qkv, w_out, w_up, w_down, norm_bias, bias_up):
    key_index = jnp.arange(LQ).astype(jnp.int32)
    allowed_q = jnp.broadcast_to((key_index[None, :] < question_lengths[:, None])[:, None, :], (NQ, LQ, LQ))
    starts = (jnp.cumsum(segment_lengths, axis=1) - segment_lengths).astype(jnp.int32)
    positions = jnp.arange(LP).astype(jnp.int32)
    seg_ids = lax.optimization_barrier(jnp.sum((positions[None, None, :] >= starts[:, :, None]).astype(jnp.int32), axis=1))
    allowed_p = seg_ids[:, :, None] == seg_ids[:, None, :]
    q_group = math.gcd(NQ, max(1, 4096 // LQ))
    p_group = math.gcd(NR, max(1, 4096 // LP))
    score_scale = 3.0 / math.sqrt(D)

    def objective(q_input, p_input, params_all):
        q_enc = encode_groups(q_input, allowed_q, tuple((member[0] for member in params_all)), q_group)
        p_enc = encode_groups(p_input, allowed_p, tuple((member[1] for member in params_all)), p_group)
        q_cls = low(q_enc[:, 0, :])
        p_cls = low(jnp.take_along_axis(p_enc, starts[:, :, None], axis=1).reshape(NP, D))
        score_tile = matmul_high(q_cls, p_cls.T) * score_scale
        row_peak = lax.optimization_barrier(jnp.max(score_tile, axis=1, keepdims=True))
        log_norm = row_peak[:, 0] + jnp.log(lax.optimization_barrier(jnp.sum(jnp.exp(score_tile - row_peak), axis=1)))
        picked = jnp.take_along_axis(score_tile, positives[:, None].astype(jnp.int32), axis=1)[:, 0]
        return (q_enc, p_enc, log_norm - picked)
    params_all = tuple((member.astype(jnp.float32) for member in (w_qkv, w_out, w_up, w_down, norm_bias, bias_up)))
    primal, pullback = jax.vjp(objective, questions.astype(jnp.float32), passages.astype(jnp.float32), params_all)
    grad_q, grad_p, grad_params = pullback((cot_questions.astype(jnp.float32), cot_passages.astype(jnp.float32), jnp.ones((NQ,), jnp.float32)))
    return (primal[0].astype(jnp.bfloat16), primal[1].astype(jnp.bfloat16), primal[2], grad_q, grad_p, grad_params[0], grad_params[1], grad_params[2], grad_params[3], grad_params[4], grad_params[5])
```

```python
import functools
import math

import jax
import jax.numpy as jnp
from jax import lax
from jax.experimental import pallas as pl
from jax.experimental.pallas import tpu as pltpu
from jax.sharding import PartitionSpec as P

HD = 64
EXTRA = 16
ROW = 256
NEG_FILL = -1000000000.0
EPSILON = 1e-06
ROOT_HALF = 0.7071067811865476
INV_ROOT_TWO_PI = 0.3989422804014327
F32 = jnp.float32
BF16 = jnp.bfloat16
MIB = 1 << 20
ANY = pl.BlockSpec(memory_space=pl.ANY)


def mm(left, right):
    return lax.dot_general(left, right, (((1,), (0,)), ((), ())), preferred_element_type=F32)


def mm_nt(left, right):
    return lax.dot_general(left, right, (((1,), (1,)), ((), ())), preferred_element_type=F32)


def mm_tn(left, right):
    return lax.dot_general(left, right, (((0,), (0,)), ((), ())), preferred_element_type=F32)


def whole(shape):
    return pl.BlockSpec(shape, lambda i: (0,) * len(shape), pipeline_mode=pl.Buffered(1))


def norm_rows(summed):
    centred = summed - jnp.mean(summed, axis=-1, keepdims=True)
    inverse = lax.rsqrt(jnp.mean(centred * centred, axis=-1, keepdims=True) + EPSILON)
    return centred * inverse, inverse


def norm_back(grad_out, gain, normed, inverse):
    scaled = grad_out * gain
    inner = (
        scaled
        - jnp.mean(scaled, axis=-1, keepdims=True)
        - normed * jnp.mean(scaled * normed, axis=-1, keepdims=True)
    )
    return inverse * inner


def col_sum(block):
    return jnp.sum(block, axis=0, keepdims=True)


def attn_fwd_kernel(dims, pack, x_ref, segc_ref, segr_ref, qkv_ref, att_ref, xhat_ref, inv_ref, wqkv_ref, wout_ref,
                    vec_ref, bup_ref, held, sem):
    npb, npa, r, wq, wo, rows_per, w1, w2 = dims
    d = x_ref.shape[1]

    @pl.when(pl.program_id(0) == 0)
    def _():
        copy = pltpu.make_async_copy(pack, held, sem)
        copy.start()
        copy.wait()
        for b in range(npb):
            rows = pl.ds(b * r, r)
            wqkv_ref[rows, :] = jnp.concatenate([held[b, a, :r, :wq] for a in range(npa)], axis=1)
            wout_ref[rows, :] = jnp.concatenate([held[b, a, :r, wq:] for a in range(npa)], axis=1)
            extra = [held[b, a, r:, :].astype(F32) for a in range(npa)]
            vec_ref[pl.ds(b * rows_per, rows_per), :] = jnp.concatenate(
                [part[:rows_per, :w1] for part in extra], axis=1)
            bup_ref[b : b + 1, :] = jnp.concatenate(
                [part[rows_per : rows_per + 1, :w2] for part in extra], axis=1)

    flat = x_ref[...]
    qkv_ref[:, :d] = ((mm(flat, wqkv_ref[:, :d]) + vec_ref[4:5, :]).astype(BF16) * BF16(HD ** -0.5))
    qkv_ref[:, d : 2 * d] = mm(flat, wqkv_ref[:, d : 2 * d]).astype(BF16)
    qkv_ref[:, 2 * d :] = (mm(flat, wqkv_ref[:, 2 * d :]) + vec_ref[5:6, :]).astype(BF16)
    blocked = jnp.where(segc_ref[0][:, 0:1] == segr_ref[0][1:2, :], 0.0, NEG_FILL)
    low_half = lax.broadcasted_iota(jnp.int32, (1, 2 * HD), 1) < HD
    keep = (low_half.astype(F32).astype(BF16), (1.0 - low_half.astype(F32)).astype(BF16))
    for p in range(d // (2 * HD)):
        lanes = slice(p * 2 * HD, (p + 1) * 2 * HD)
        q2 = qkv_ref[:, lanes]
        k2 = qkv_ref[:, d + p * 2 * HD : d + (p + 1) * 2 * HD]
        v2 = qkv_ref[:, 2 * d + p * 2 * HD : 2 * d + (p + 1) * 2 * HD]
        parts = []
        for h in range(2):
            scores = mm_nt(q2 * keep[h], k2) + blocked
            terms = jnp.exp(scores - jnp.max(scores, axis=-1, keepdims=True))
            total = jnp.sum(terms, axis=-1, keepdims=True)
            prob = (terms / total).astype(BF16)
            parts.append(mm(prob, v2))
        att_ref[:, lanes] = jnp.where(low_half, parts[0], parts[1]).astype(BF16)
    branch = mm(att_ref[...], wout_ref[...]) + vec_ref[6:7, :]
    normed, inverse = norm_rows(flat.astype(F32) + branch)
    xhat_ref[...] = normed
    inv_ref[...] = inverse


def attn_fwd(dims, pack, x, segc, segr):
    npb, npa, r, wq, wo, rows_per, w1, w2 = dims
    tokens, d = x.shape
    steps = tokens // ROW
    ff = w2 * npa * npb
    row = lambda width: pl.BlockSpec((ROW, width), lambda i: (i, 0))
    return pl.pallas_call(
        functools.partial(attn_fwd_kernel, dims),
        grid=(steps,),
        in_specs=[ANY, row(d), pl.BlockSpec((1, ROW, 2), lambda i: (i, 0, 0)),
                  pl.BlockSpec((1, 2, ROW), lambda i: (i, 0, 0))],
        out_specs=[row(3 * d), row(d), row(d), row(1), whole((d, 3 * d)), whole((d, d)), whole((8, d)),
                   whole((npb, ff // npb))],
        out_shape=[
            jax.ShapeDtypeStruct((tokens, 3 * d), BF16),
            jax.ShapeDtypeStruct((tokens, d), BF16),
            jax.ShapeDtypeStruct((tokens, d), F32),
            jax.ShapeDtypeStruct((tokens, 1), F32),
            jax.ShapeDtypeStruct((d, 3 * d), BF16),
            jax.ShapeDtypeStruct((d, d), BF16),
            jax.ShapeDtypeStruct((8, d), F32),
            jax.ShapeDtypeStruct((npb, ff // npb), F32),
        ],
        scratch_shapes=[pltpu.VMEM(pack.shape, BF16), pltpu.SemaphoreType.DMA],
        compiler_params=pltpu.CompilerParams(vmem_limit_bytes=58 * MIB),
        cost_estimate=pl.CostEstimate(flops=2 * tokens * d * (4 * d + 8 * ROW), transcendentals=0,
                                      bytes_accessed=40 * MIB),
        name="attn_fwd",
    )(pack, x, segc, segr)


def load_ffn(pack, up, down, sems):
    npb, npa, _, rows, c = pack.shape
    r = up.shape[0] // npb
    dr = up.shape[0] // npa
    dc = up.shape[1] // npb
    for b in range(npb):
        for a in range(npa):
            pltpu.make_async_copy(pack.at[b, a, 0], up.at[pl.ds(b * r, r), pl.ds(a * c, c)], sems.at[0]).start()
    for b in range(npb):
        for a in range(npa):
            for j in range(dc // c):
                pltpu.make_async_copy(
                    pack.at[b, a, 1, pl.ds(j * dr, dr), :],
                    down.at[pl.ds(a * dr, dr), pl.ds(b * dc + j * c, c)], sems.at[1]).start()
    pltpu.make_async_copy(up, up, sems.at[0]).wait()
    pltpu.make_async_copy(down, down, sems.at[1]).wait()


def ffn_fwd_kernel(spot_ref, pack, xhat_ref, vec_ref, bup_ref, act_ref, slope_ref, norm_ref, inv_ref, enc_ref, cls_ref,
                   up, down, held, sems):
    step = pl.program_id(0)

    @pl.when(step == 0)
    def _():
        load_ffn(pack, up, down, sems)

    ff = up.shape[1]
    tiles = bup_ref.shape[0]
    width = ff // tiles
    first_norm = xhat_ref[...] * vec_ref[0:1, :] + vec_ref[1:2, :]
    first_low = first_norm.astype(BF16)
    total = first_norm + vec_ref[7:8, :]
    for t in range(tiles):
        cols = slice(t * width, (t + 1) * width)
        hidden = mm(first_low, up[:, cols]) + bup_ref[t : t + 1, :]
        cdf = 0.5 + 0.5 * lax.erf(hidden * ROOT_HALF)
        act = (hidden * cdf).astype(BF16)
        act_ref[:, cols] = act
        slope_ref[:, cols] = (cdf + hidden * (jnp.exp(-0.5 * hidden * hidden) * INV_ROOT_TWO_PI)).astype(BF16)
        total = total + mm_nt(act, down[:, cols])
    normed, inverse = norm_rows(total)
    norm_ref[...] = normed
    inv_ref[...] = inverse
    enc = (normed * vec_ref[2:3, :] + vec_ref[3:4, :]).astype(BF16)
    enc_ref[...] = enc
    held[...] = enc.astype(F32)
    for j in range(cls_ref.shape[1]):
        cls_ref[0, j : j + 1, :] = held[pl.ds(spot_ref[step, j], 1), :]


def ffn_fwd(spots, pack, xhat, vec, bup):
    tokens, d = xhat.shape
    steps, per_row = spots.shape
    ff = bup.shape[0] * bup.shape[1]
    row = lambda width: pl.BlockSpec((ROW, width), lambda i: (i, 0))
    return pl.pallas_call(
        ffn_fwd_kernel,
        grid=(steps,),
        in_specs=[pl.BlockSpec(memory_space=pltpu.SMEM), ANY, row(d), whole(vec.shape), whole(bup.shape)],
        out_specs=[row(ff), row(ff), row(d), row(1), row(d), pl.BlockSpec((1, per_row, d), lambda i: (i, 0, 0))],
        out_shape=[
            jax.ShapeDtypeStruct((tokens, ff), BF16),
            jax.ShapeDtypeStruct((tokens, ff), BF16),
            jax.ShapeDtypeStruct((tokens, d), F32),
            jax.ShapeDtypeStruct((tokens, 1), F32),
            jax.ShapeDtypeStruct((tokens, d), BF16),
            jax.ShapeDtypeStruct((steps, per_row, d), F32),
        ],
        scratch_shapes=[pltpu.VMEM((d, ff), BF16), pltpu.VMEM((d, ff), BF16), pltpu.VMEM((ROW, d), F32),
                        pltpu.SemaphoreType.DMA((2,))],
        compiler_params=pltpu.CompilerParams(vmem_limit_bytes=58 * MIB),
        cost_estimate=pl.CostEstimate(flops=4 * tokens * d * ff, transcendentals=0, bytes_accessed=40 * MIB),
        name="ffn_fwd",
    )(spots, pack, xhat, vec, bup)


def loss_kernel(scale, q_all, p_all, q_own, p_own, hit_all, hit_own, loss_ref, gq_ref, gp_ref):
    def split_mm(dot, left, right):
        high = left.astype(BF16)
        rest = left - high.astype(F32)
        mid = rest.astype(BF16)
        tail = (rest - mid.astype(F32)).astype(BF16)
        return dot(high, right) + dot(mid, right) + dot(tail, right)

    def log_norm(scores):
        peak = jnp.max(scores, axis=1, keepdims=True)
        return peak + jnp.log(jnp.sum(jnp.exp(scores - peak), axis=1, keepdims=True))

    full = mm_nt(q_all[...], p_all[...]) * scale
    norm_all = log_norm(full)
    own_rows = mm_nt(q_own[...], p_all[...]) * scale
    norm_own = log_norm(own_rows)
    hits = lax.broadcasted_iota(jnp.int32, own_rows.shape, 1) == hit_own[...]
    loss_ref[...] = norm_own - jnp.sum(jnp.where(hits, own_rows, 0.0), axis=1, keepdims=True)
    tile = jnp.exp(own_rows - norm_own) - jnp.where(hits, 1.0, 0.0)
    gq_ref[...] = split_mm(mm, tile, p_all[...]) * scale
    own_cols = mm_nt(q_all[...], p_own[...]) * scale
    hits = lax.broadcasted_iota(jnp.int32, own_cols.shape, 1) == hit_all[...]
    tile = jnp.exp(own_cols - norm_all) - jnp.where(hits, 1.0, 0.0)
    gp_ref[...] = split_mm(mm_tn, tile, q_all[...]) * scale


def loss_part(q_all, p_all, q_own, p_own, hit_all, hit_own):
    d = q_all.shape[1]
    return pl.pallas_call(
        functools.partial(loss_kernel, 3.0 / math.sqrt(d)),
        out_shape=[
            jax.ShapeDtypeStruct((q_own.shape[0], 1), F32),
            jax.ShapeDtypeStruct(q_own.shape, F32),
            jax.ShapeDtypeStruct(p_own.shape, F32),
        ],
        compiler_params=pltpu.CompilerParams(vmem_limit_bytes=58 * MIB),
        name="loss_part",
    )(q_all, p_all, q_own, p_own, hit_all, hit_own)


def ffn_bwd_kernel(steps, spot_ref, pack, cot_ref, gcls_ref, norm_ref, inv2_ref, act_ref, slope_ref, xhat_ref, inv1_ref,
                   vec_ref, dh_ref, dup_ref, ddown_ref, gvec_ref, gbup_ref,
                   up, down, held, first_t, down_t, hidden_all, act_all, sems):
    step = pl.program_id(0)
    tiles = gbup_ref.shape[0]
    ff = up.shape[1]
    width = ff // tiles

    @pl.when(step == 0)
    def _():
        load_ffn(pack, up, down, sems)
        gvec_ref[...] = jnp.zeros_like(gvec_ref)
        gbup_ref[...] = jnp.zeros_like(gbup_ref)

    @pl.when(step < steps)
    def _():
        held[...] = cot_ref[...].astype(F32)
        for j in range(gcls_ref.shape[1]):
            spot = pl.ds(spot_ref[step, j], 1)
            held[spot, :] = held[spot, :] + gcls_ref[0, j : j + 1, :]
        grad_out = held[...]
        normed = norm_ref[...]
        gvec_ref[2:3, :] += col_sum(grad_out * normed)
        gvec_ref[3:4, :] += col_sum(grad_out)
        grad_two = norm_back(grad_out, vec_ref[2:3, :], normed, inv2_ref[...])
        down_low = grad_two.astype(BF16)
        gvec_ref[7:8, :] += col_sum(down_low.astype(F32))
        tok = pl.ds(pl.multiple_of(step * ROW, ROW), ROW)
        total = grad_two
        for t in range(tiles):
            cols = slice(t * width, (t + 1) * width)
            hidden = (mm(down_low, down[:, cols]) * slope_ref[:, cols].astype(F32)).astype(BF16)
            hidden_all[tok, cols] = hidden
            gbup_ref[t : t + 1, :] += col_sum(hidden.astype(F32))
            total = total + mm_nt(hidden, up[:, cols])
        act_all[tok, :] = act_ref[...]
        xhat = xhat_ref[...]
        gvec_ref[0:1, :] += col_sum(total * xhat)
        gvec_ref[1:2, :] += col_sum(total)
        dh_ref[...] = norm_back(total, vec_ref[0:1, :], xhat, inv1_ref[...])
        first_low = (xhat * vec_ref[0:1, :] + vec_ref[1:2, :]).astype(BF16)
        for s in range(steps):
            @pl.when(step == s)
            def _():
                first_t[:, s * ROW : (s + 1) * ROW] = first_low.T
                down_t[:, s * ROW : (s + 1) * ROW] = down_low.T

    npb, npa, r, c = (dup_ref.shape[0], ddown_ref.shape[1], dup_ref.shape[2], dup_ref.shape[3])
    rows = ddown_ref.shape[2]
    d = up.shape[0]
    dr = d // npa
    part = ff // npb

    for b in range(npb):
        @pl.when(step == steps + b)
        def _():
            cols = slice(b * part, (b + 1) * part)
            got = mm(first_t[...], hidden_all[:, cols]).astype(BF16)
            for j in range(part // c):
                for e in range(npb):
                    dup_ref[e, j] = got[e * r : (e + 1) * r, j * c : (j + 1) * c]
            got = mm(down_t[...], act_all[:, cols]).astype(BF16)
            for j in range(part // c):
                for a in range(npa):
                    ddown_ref[0, a, j * dr : (j + 1) * dr, :] = got[a * dr : (a + 1) * dr, j * c : (j + 1) * c]


def ffn_bwd(spots, pack, cot, gcls, norm2, inv2, act, slope, xhat, inv1, vec, bup_shape):
    tokens, d = xhat.shape
    steps, per_row = spots.shape
    npb, npa, _, rows, c = pack.shape
    ff = act.shape[1]
    last = lambda i: jnp.minimum(i, steps - 1)
    row = lambda width: pl.BlockSpec((ROW, width), lambda i: (last(i), 0))
    after = lambda i: jnp.maximum(i - steps, 0)
    return pl.pallas_call(
        functools.partial(ffn_bwd_kernel, steps),
        grid=(steps + npb,),
        in_specs=[pl.BlockSpec(memory_space=pltpu.SMEM), ANY, row(d),
                  pl.BlockSpec((1, per_row, d), lambda i: (last(i), 0, 0)), row(d), row(1), row(ff), row(ff), row(d), row(1),
                  whole(vec.shape)],
        out_specs=[row(d), pl.BlockSpec((npb, npa // npb, rows, c), lambda i: (0, after(i), 0, 0)),
                   pl.BlockSpec((1, npa, rows, c), lambda i: (after(i), 0, 0, 0)), whole(vec.shape), whole(bup_shape)],
        out_shape=[
            jax.ShapeDtypeStruct((tokens, d), F32),
            jax.ShapeDtypeStruct((npb, npa, rows, c), BF16),
            jax.ShapeDtypeStruct((npb, npa, rows, c), BF16),
            jax.ShapeDtypeStruct(vec.shape, F32),
            jax.ShapeDtypeStruct(bup_shape, F32),
        ],
        scratch_shapes=[pltpu.VMEM((d, ff), BF16), pltpu.VMEM((d, ff), BF16), pltpu.VMEM((ROW, d), F32),
                        pltpu.VMEM((d, tokens), BF16), pltpu.VMEM((d, tokens), BF16), pltpu.VMEM((tokens, ff), BF16),
                        pltpu.VMEM((tokens, ff), BF16), pltpu.SemaphoreType.DMA((2,))],
        compiler_params=pltpu.CompilerParams(vmem_limit_bytes=60 * MIB),
        cost_estimate=pl.CostEstimate(flops=8 * tokens * d * ff, transcendentals=0, bytes_accessed=60 * MIB),
        name="ffn_bwd",
    )(spots, pack, cot, gcls, norm2, inv2, act, slope, xhat, inv1, vec)


def attn_bwd_kernel(dims, steps, dh_ref, qkv_ref, att_ref, x_ref, segc_ref, segr_ref, wqkv_ref, wout_ref, gvec_in, gbup_in,
                    gx_ref, dpack_ref, x_t, att_t, proj, branch, gvec):
    npb, npa, r, wq, wo, rows_per, w1, w2 = dims
    step = pl.program_id(0)
    d = x_ref.shape[1]

    @pl.when(step == 0)
    def _():
        gvec[...] = gvec_in[...]

    @pl.when(step < steps)
    def _():
        dh = dh_ref[...]
        low = dh.astype(BF16)
        tok = pl.ds(pl.multiple_of(step * ROW, ROW), ROW)
        branch[tok, :] = low
        gvec[6:7, :] += col_sum(low.astype(F32))
        att_grad = mm_nt(low, wout_ref[...]).astype(BF16)
        blocked = jnp.where(segc_ref[0][:, 1:2] == segr_ref[0][0:1, :], 0.0, NEG_FILL)
        low_half = lax.broadcasted_iota(jnp.int32, (1, 2 * HD), 1) < HD
        keep = (low_half.astype(F32).astype(BF16), (1.0 - low_half.astype(F32)).astype(BF16))
        for p in range(d // (2 * HD)):
            lanes = slice(p * 2 * HD, (p + 1) * 2 * HD)
            k_lanes = slice(d + p * 2 * HD, d + (p + 1) * 2 * HD)
            v_lanes = slice(2 * d + p * 2 * HD, 2 * d + (p + 1) * 2 * HD)
            q2 = qkv_ref[:, lanes]
            k2 = qkv_ref[:, k_lanes]
            v2 = qkv_ref[:, v_lanes]
            g2 = att_grad[:, lanes]
            dq, dk, dv = [], [], []
            for h in range(2):
                scores = mm_nt(k2 * keep[h], q2) + blocked
                terms = jnp.exp(scores - jnp.max(scores, axis=0, keepdims=True))
                prob = terms / jnp.sum(terms, axis=0, keepdims=True)
                weighed = prob * mm_nt(v2 * keep[h], g2)
                sgrad = (weighed - prob * jnp.sum(weighed, axis=0, keepdims=True)).astype(BF16)
                dv.append(mm(prob.astype(BF16), g2))
                dk.append(mm(sgrad, q2))
                dq.append(mm_tn(sgrad, k2))
            proj[tok, lanes] = (jnp.where(low_half, dq[0], dq[1]) * (HD ** -0.5)).astype(BF16)
            proj[tok, k_lanes] = jnp.where(low_half, dk[0], dk[1]).astype(BF16)
            proj[tok, v_lanes] = jnp.where(low_half, dv[0], dv[1]).astype(BF16)
        gvec[4:5, :] += col_sum(proj[tok, :d].astype(F32))
        gvec[5:6, :] += col_sum(proj[tok, 2 * d :].astype(F32))
        gx_ref[...] = mm_nt(proj[tok, :], wqkv_ref[...]) + dh
        for s in range(steps):
            @pl.when(step == s)
            def _():
                x_t[:, s * ROW : (s + 1) * ROW] = x_ref[...].T
                att_t[:, s * ROW : (s + 1) * ROW] = att_ref[...].T

    @pl.when(step == steps)
    def _():
        wide = jnp.concatenate([mm(x_t[...], proj[:, g * d : (g + 1) * d]).astype(BF16) for g in range(3)], axis=1)
        out = mm(att_t[...], branch[...]).astype(BF16)
        for a in range(npa):
            block = jnp.concatenate([wide[:, a * wq : (a + 1) * wq], out[:, a * wo : (a + 1) * wo]], axis=1)
            for b in range(npb):
                dpack_ref[b, a, :r, :] = block[b * r : (b + 1) * r, :]
        c = wq + wo

        def widen(piece):
            if piece.shape[1] == c:
                return piece
            return jnp.concatenate([piece, jnp.zeros((piece.shape[0], c - piece.shape[1]), F32)], axis=1)

        for b in range(npb):
            for a in range(npa):
                rows = [widen(gvec[b * rows_per : (b + 1) * rows_per, a * w1 : (a + 1) * w1]),
                        widen(gbup_in[b : b + 1, a * w2 : (a + 1) * w2]),
                        jnp.zeros((EXTRA - 1 - rows_per, c), F32)]
                dpack_ref[b, a, r:, :] = jnp.concatenate(rows, axis=0).astype(BF16)


def attn_bwd(dims, dh, qkv, att, x, segc, segr, wqkv, wout, gvec, gbup):
    npb, npa, r, wq, wo, rows_per, w1, w2 = dims
    tokens, d = x.shape
    steps = tokens // ROW
    last = lambda i: jnp.minimum(i, steps - 1)
    row = lambda width: pl.BlockSpec((ROW, width), lambda i: (last(i), 0))
    return pl.pallas_call(
        functools.partial(attn_bwd_kernel, dims, steps),
        grid=(steps + 1,),
        in_specs=[row(d), row(3 * d), row(d), row(d), pl.BlockSpec((1, ROW, 2), lambda i: (last(i), 0, 0)),
                  pl.BlockSpec((1, 2, ROW), lambda i: (last(i), 0, 0)), whole(wqkv.shape), whole(wout.shape),
                  whole(gvec.shape), whole(gbup.shape)],
        out_specs=[row(d), whole((npb, npa, r + EXTRA, wq + wo))],
        out_shape=[
            jax.ShapeDtypeStruct((tokens, d), F32),
            jax.ShapeDtypeStruct((npb, npa, r + EXTRA, wq + wo), BF16),
        ],
        scratch_shapes=[pltpu.VMEM((d, tokens), BF16), pltpu.VMEM((d, tokens), BF16), pltpu.VMEM((tokens, 3 * d), BF16),
                        pltpu.VMEM((tokens, d), BF16), pltpu.VMEM(gvec.shape, F32)],
        compiler_params=pltpu.CompilerParams(vmem_limit_bytes=60 * MIB),
        cost_estimate=pl.CostEstimate(flops=4 * tokens * d * (4 * d + 10 * ROW), transcendentals=0,
                                      bytes_accessed=40 * MIB),
        name="attn_bwd",
    )(dh, qkv, att, x, segc, segr, wqkv, wout, gvec, gbup)


class Blocks:
    def __init__(self, npb, npa, d, ff):
        self.npb, self.npa, self.d, self.ff = npb, npa, d, ff
        self.r, self.wq, self.wo, self.c = d // npb, 3 * d // npa, d // npa, ff // npa
        self.dr, self.dc = d // npa, ff // npb
        self.rows_per, self.w1, self.w2 = 8 // npb, d // npa, ff // (npa * npb)
        self.direct = self.c % 128 == 0 and self.r % 16 == 0 and self.dr % 16 == 0
        if self.direct:
            self.dims = (npb, npa, self.r, self.wq, self.wo, self.rows_per, self.w1, self.w2)
        else:
            self.dims = (1, 1, d, 3 * d, d, 8, d, ff)

    def pack(self, w_qkv, w_out, w_up, w_down, norm_bias, bias_up):
        c = self.wq + self.wo
        vec = jnp.pad(norm_bias, ((0, 0), (0, 0), (0, c - self.w1)))
        bup = jnp.pad(bias_up[:, None, :], ((0, 0), (0, EXTRA - 1 - self.rows_per), (0, c - self.w2)))
        attn = jnp.concatenate([jnp.concatenate([w_qkv, w_out], axis=2), vec, bup], axis=1)
        down_t = jnp.swapaxes(w_down, 1, 2)
        down = jnp.concatenate([down_t[:, :, j : j + self.c] for j in range(0, self.dc, self.c)], axis=1)
        return attn, jnp.stack([w_up, down], axis=1)

    def from_blocks(self, attn, ffn):
        if self.direct:
            return attn, ffn
        d, ff, r = self.d, self.ff, self.r
        rows = lambda part, height: part.transpose(0, 2, 1, 3).reshape(height, -1)
        qkv = rows(attn[:, :, :r, : self.wq], d)
        out = rows(attn[:, :, :r, self.wq :], d)
        vec = rows(attn[:, :, r : r + self.rows_per, : self.w1], 8)
        bup = attn[:, :, r + self.rows_per, : self.w2].reshape(1, ff)
        vec = jnp.pad(vec, ((0, 0), (0, 3 * d)))
        bup = jnp.pad(bup, ((0, EXTRA - 9), (0, 4 * d - ff)))
        wide = jnp.concatenate([jnp.concatenate([qkv, out], axis=1), vec, bup], axis=0)
        up = rows(ffn[:, :, 0], d)
        pieces = self.dc // self.c
        down = ffn[:, :, 1].reshape(self.npb, self.npa, pieces, self.dr, self.c)
        down = down.transpose(1, 3, 0, 2, 4).reshape(d, ff)
        return wide[None, None], jnp.stack([up, down])[None, None]

    def to_blocks(self, attn, up, down):
        if self.direct:
            return attn, up, down
        d, ff, npb, npa = self.d, self.ff, self.npb, self.npa
        blocks = lambda part, height: part.reshape(npb, height, npa, -1).transpose(0, 2, 1, 3)
        wide = attn[0, 0]
        c = self.wq + self.wo
        main = jnp.concatenate([blocks(wide[:d, : 3 * d], self.r), blocks(wide[:d, 3 * d :], self.r)], axis=3)
        vec = blocks(wide[d : d + 8, :d], self.rows_per)
        vec = jnp.pad(vec, ((0, 0), (0, 0), (0, 0), (0, c - self.w1)))
        bup = wide[d + 8, :ff].reshape(npb, npa, 1, self.w2)
        bup = jnp.pad(bup, ((0, 0), (0, 0), (0, EXTRA - 1 - self.rows_per), (0, c - self.w2)))
        pieces = self.dc // self.c
        down = down[0, 0].reshape(npa, self.dr, npb, pieces, self.c).transpose(2, 0, 3, 1, 4)
        down = down.reshape(npb, npa, pieces * self.dr, self.c)
        return jnp.concatenate([main, vec, bup], axis=2), blocks(up[0, 0], self.r), down

    def unpack(self, attn, up, down):
        r = self.r
        down = jnp.concatenate([down[:, j * self.dr : (j + 1) * self.dr] for j in range(self.dc // self.c)], axis=2)
        return (attn[:, :r, : self.wq], attn[:, :r, self.wq :], up, jnp.swapaxes(down, 1, 2),
                attn[:, r : r + self.rows_per, : self.w1], attn[:, r + self.rows_per, : self.w2])


BOTH = ("pb", "pa")


def body(questions, passages, cot_questions, cot_passages, question_lengths, segment_lengths, positives, w_qkv, w_out, w_up,
         w_down, norm_bias, bias_up):
    q_count, q_len, d = questions.shape
    row_count, row_len, _ = passages.shape
    segs = segment_lengths.shape[1]
    npb, npa = lax.axis_size("pb"), lax.axis_size("pa")
    size = Blocks(npb, npa, d, bias_up.shape[1] * npb * npa)
    dims = size.dims
    device = lax.axis_index("pb") * npa + lax.axis_index("pa")

    attn_pack, ffn_pack = size.pack(w_qkv, w_out, w_up, w_down, norm_bias, bias_up)
    attn_all = lax.all_gather(attn_pack, BOTH, axis=0).reshape((npb, npa) + attn_pack.shape)
    ffn_all = lax.all_gather(ffn_pack, BOTH, axis=0).reshape((npb, npa) + ffn_pack.shape)
    attn_w, ffn_w = zip(*[size.from_blocks(attn_all[:, :, e], ffn_all[:, :, e]) for e in range(2)])

    per_row = ROW // q_len
    q_rows = q_count // per_row
    token = jnp.arange(ROW, dtype=jnp.int32)
    q_seg = jnp.broadcast_to(token // q_len, (q_rows, ROW))
    q_valid = (token % q_len)[None, :] < jnp.repeat(question_lengths.reshape(q_rows, per_row), q_len, axis=1)
    starts = jnp.cumsum(segment_lengths, axis=1) - segment_lengths
    p_seg = jnp.sum((token[None, None, :] >= starts[:, :, None]).astype(jnp.int32), axis=1)
    seg_pairs = (jnp.stack([q_seg, jnp.where(q_valid, q_seg, -1)], axis=1), jnp.stack([p_seg, p_seg], axis=1))
    segr = seg_pairs
    segc = tuple(jnp.swapaxes(pair, 1, 2) for pair in seg_pairs)
    spots = (jnp.broadcast_to(jnp.arange(per_row, dtype=jnp.int32) * q_len, (q_rows, per_row)), starts)
    xs = (questions.reshape(-1, d), passages.reshape(-1, d))
    cots = (cot_questions.reshape(-1, d), cot_passages.reshape(-1, d))

    half = [attn_fwd(dims, attn_w[e], xs[e], segc[e], segr[e]) for e in range(2)]
    done = [ffn_fwd(spots[e], ffn_w[e], half[e][2], half[e][6], half[e][7]) for e in range(2)]
    q_own = done[0][5].reshape(q_count, d).astype(BF16)
    p_own = done[1][5].reshape(row_count * segs, d).astype(BF16)

    heads = lax.all_gather(jnp.concatenate([q_own, p_own]), BOTH, axis=0)
    q_all = heads[:, :q_count].reshape(-1, d)
    p_all = heads[:, q_count:].reshape(-1, d)
    hit_all = lax.all_gather(positives, "pb", axis=0, tiled=True)[:, None]
    hit_own = lax.dynamic_slice_in_dim(hit_all, device * q_count, q_count)
    losses, gq, gp = loss_part(q_all, p_all, q_own, p_own, hit_all - device * (row_count * segs), hit_own)
    gcls = (gq.reshape(q_rows, per_row, d), gp.reshape(row_count, segs, d))

    grads = []
    for e in range(2):
        qkv, att, xhat, inv1, wqkv, wout, vec, bup = half[e]
        act, slope, norm2, inv2, _, _ = done[e]
        dh, dup, ddown, gvec, gbup = ffn_bwd(spots[e], ffn_w[e], cots[e], gcls[e], norm2, inv2, act, slope, xhat, inv1, vec,
                                             bup.shape)
        gx, dattn = attn_bwd(dims, dh, qkv, att, xs[e], segc[e], segr[e], wqkv, wout, gvec, gbup)
        grads.append((gx, size.to_blocks(dattn, dup, ddown)))

    def scatter(index):
        both = jnp.stack([grads[e][1][index] for e in range(2)], axis=2)
        flat = both.reshape((npb * npa,) + both.shape[2:])
        return lax.psum_scatter(flat, BOTH, scatter_dimension=0, tiled=False).astype(F32)

    outs = size.unpack(scatter(0), scatter(1), scatter(2))
    return (
        done[0][4].reshape(questions.shape),
        done[1][4].reshape(passages.shape),
        losses[:, 0],
        grads[0][0].reshape(questions.shape),
        grads[1][0].reshape(passages.shape),
    ) + outs


def solution(mesh):
    rows = P(BOTH, None, None)
    shard = P(None, "pb", "pa")
    vector = P(None, BOTH)
    in_specs = (rows, rows, rows, rows, P(BOTH), P(BOTH, None), P("pb"), shard, shard, shard, shard, shard, vector)
    out_specs = (rows, rows, P(BOTH), rows, rows, shard, shard, shard, shard, shard, vector)
    return jax.shard_map(body, mesh=mesh, in_specs=in_specs, out_specs=out_specs, check_vma=False)
```

```python
import functools
import math

import jax
import jax.numpy as jnp
from jax import lax
from jax.experimental import pallas as pl
from jax.experimental.pallas import tpu as pltpu
from jax.sharding import PartitionSpec as P

HD = 64
EXTRA = 16
ROW = 256
FFN_ROW = 256
NEG_FILL = -1000000000.0
EPSILON = 1e-06
ROOT_HALF = 0.7071067811865476
INV_ROOT_TWO_PI = 0.3989422804014327
F32 = jnp.float32
BF16 = jnp.bfloat16
MIB = 1 << 20
ANY = pl.BlockSpec(memory_space=pl.ANY)
SMEM = pl.BlockSpec(memory_space=pltpu.SMEM)


def mm(left, right):
    return lax.dot_general(left, right, (((1,), (0,)), ((), ())), preferred_element_type=F32)


def mm_nt(left, right):
    return lax.dot_general(left, right, (((1,), (1,)), ((), ())), preferred_element_type=F32)


def mm_tn(left, right):
    return lax.dot_general(left, right, (((0,), (0,)), ((), ())), preferred_element_type=F32)


def whole(shape):
    return pl.BlockSpec(shape, lambda i: (0,) * len(shape), pipeline_mode=pl.Buffered(1))


def norm_rows(summed):
    centred = summed - jnp.mean(summed, axis=-1, keepdims=True)
    inverse = lax.rsqrt(jnp.mean(centred * centred, axis=-1, keepdims=True) + EPSILON)
    return centred * inverse, inverse


def norm_back(grad_out, gain, normed, inverse):
    scaled = grad_out * gain
    inner = (
        scaled
        - jnp.mean(scaled, axis=-1, keepdims=True)
        - normed * jnp.mean(scaled * normed, axis=-1, keepdims=True)
    )
    return inverse * inner


def col_sum(block):
    return jnp.sum(block, axis=0, keepdims=True)


class Place:
    def __init__(self, npb, npa, first, into):
        self.npb, self.npa, self.first, self.into = npb, npa, first, into
        self.count = 1 if first is None else 8 if into else 2
        self.lead = (npb, npa) if first is None else (4,) if into else (2, 2, 4)

    def blocks(self, spot):
        if self.first is None:
            return [(0, (b, a), b, a) for b in range(self.npb) for a in range(self.npa)]
        y, core, z, x = (spot[k] for k in range(4))
        found = []
        for core_d in range(2):
            for second in range(2):
                for first in range(2):
                    for z_d in range(4):
                        y_d, x_d = (first, second) if self.first == "y" else (second, first)
                        index = core_d * 4 + second * 2 + first if self.into else core_d
                        lead = (z_d,) if self.into else (first, second, z_d)
                        b = lax.bitwise_xor(y, y_d) * 2 + lax.bitwise_xor(core, core_d)
                        a = lax.bitwise_xor(z, z_d) * 2 + lax.bitwise_xor(x, x_d)
                        found.append((index, lead, b, a))
        return found


def span(index, length):
    start = index * length
    if isinstance(start, int):
        return pl.ds(start, length)
    return pl.ds(pl.multiple_of(start, math.gcd(length, 1 << 20)), length)


def lane_span(index, stride, base, length):
    start = index * stride + base
    if isinstance(start, int):
        return pl.ds(start, length)
    return pl.ds(pl.multiple_of(start, 128), length)


def attn_fwd_kernel(dims, place, here_ref, *refs):
    packs, refs = refs[: place.count], refs[place.count :]
    (x_ref, segc_ref, segr_ref, qkv_ref, att_ref, xhat_ref, inv_ref, wqkv_ref, wout_ref, vec_ref, bup_ref, held, sem) = refs
    npb, npa, r, wq, wo, rows_per, w1, w2 = dims
    d = x_ref.shape[1]

    @pl.when(pl.program_id(0) == 0)
    def _():
        for index, lead, b, a in place.blocks(here_ref):
            pltpu.make_async_copy(packs[index].at[lead], held.at[b, a], sem).start()
        pltpu.make_async_copy(held, held, sem).wait()
        for b in range(npb):
            rows = pl.ds(b * r, r)
            wqkv_ref[rows, :] = jnp.concatenate([held[b, a, :r, :wq] for a in range(npa)], axis=1)
            wout_ref[rows, :] = jnp.concatenate([held[b, a, :r, wq:] for a in range(npa)], axis=1)
            extra = [held[b, a, r:, :].astype(F32) for a in range(npa)]
            vec_ref[pl.ds(b * rows_per, rows_per), :] = jnp.concatenate(
                [part[:rows_per, :w1] for part in extra], axis=1)
            bup_ref[b : b + 1, :] = jnp.concatenate(
                [part[rows_per : rows_per + 1, :w2] for part in extra], axis=1)

    flat = x_ref[...]
    qkv_ref[:, :d] = ((mm(flat, wqkv_ref[:, :d]) + vec_ref[4:5, :]).astype(BF16) * BF16(HD ** -0.5))
    qkv_ref[:, d : 2 * d] = mm(flat, wqkv_ref[:, d : 2 * d]).astype(BF16)
    qkv_ref[:, 2 * d :] = (mm(flat, wqkv_ref[:, 2 * d :]) + vec_ref[5:6, :]).astype(BF16)
    blocked = jnp.where(segc_ref[0][:, 0:1] == segr_ref[0][1:2, :], 0.0, NEG_FILL)
    low_half = lax.broadcasted_iota(jnp.int32, (1, 2 * HD), 1) < HD
    keep = (low_half.astype(F32).astype(BF16), (1.0 - low_half.astype(F32)).astype(BF16))
    for p in range(d // (2 * HD)):
        lanes = slice(p * 2 * HD, (p + 1) * 2 * HD)
        q2 = qkv_ref[:, lanes]
        k2 = qkv_ref[:, d + p * 2 * HD : d + (p + 1) * 2 * HD]
        v2 = qkv_ref[:, 2 * d + p * 2 * HD : 2 * d + (p + 1) * 2 * HD]
        parts = []
        for h in range(2):
            scores = mm_nt(q2 * keep[h], k2) + blocked
            terms = jnp.exp(scores - jnp.max(scores, axis=-1, keepdims=True))
            total = jnp.sum(terms, axis=-1, keepdims=True)
            prob = (terms * (1.0 / total)).astype(BF16)
            parts.append(mm(prob, v2))
        att_ref[:, lanes] = jnp.where(low_half, parts[0], parts[1]).astype(BF16)
    branch = mm(att_ref[...], wout_ref[...]) + vec_ref[6:7, :]
    normed, inverse = norm_rows(flat.astype(F32) + branch)
    xhat_ref[...] = normed
    inv_ref[...] = inverse


def attn_fwd(dims, place, here, packs, x, segc, segr):
    npb, npa, r, wq, wo, rows_per, w1, w2 = dims
    tokens, d = x.shape
    steps = tokens // ROW
    ff = w2 * npa * npb
    row = lambda width: pl.BlockSpec((ROW, width), lambda i: (i, 0))
    return pl.pallas_call(
        functools.partial(attn_fwd_kernel, dims, place),
        grid=(steps,),
        in_specs=[SMEM] + [ANY] * place.count + [row(d), pl.BlockSpec((1, ROW, 2), lambda i: (i, 0, 0)),
                  pl.BlockSpec((1, 2, ROW), lambda i: (i, 0, 0))],
        out_specs=[row(3 * d), row(d), row(d), row(1), whole((d, 3 * d)), whole((d, d)), whole((8, d)),
                   whole((npb, ff // npb))],
        out_shape=[
            jax.ShapeDtypeStruct((tokens, 3 * d), BF16),
            jax.ShapeDtypeStruct((tokens, d), BF16),
            jax.ShapeDtypeStruct((tokens, d), F32),
            jax.ShapeDtypeStruct((tokens, 1), F32),
            jax.ShapeDtypeStruct((d, 3 * d), BF16),
            jax.ShapeDtypeStruct((d, d), BF16),
            jax.ShapeDtypeStruct((8, d), F32),
            jax.ShapeDtypeStruct((npb, ff // npb), F32),
        ],
        scratch_shapes=[pltpu.VMEM((npb, npa, r + EXTRA, wq + wo), BF16), pltpu.SemaphoreType.DMA],
        compiler_params=pltpu.CompilerParams(vmem_limit_bytes=58 * MIB),
        cost_estimate=pl.CostEstimate(flops=2 * tokens * d * (4 * d + 8 * ROW), transcendentals=0,
                                      bytes_accessed=40 * MIB),
        name="attn_fwd",
    )(here, *packs, x, segc, segr)


class FfnPlace:
    def __init__(self, up, down=None, e=None):
        self.up, self.down, self.apart, self.e = up, down or up, down is not None, e
        self.npb, self.npa = up.npb, up.npa
        self.count = up.count + down.count if down else up.count

    def shapes(self, d, ff):
        block = (d // self.npb * (1 if self.apart else 2), ff // self.npa)
        places = [self.up, self.down] if self.apart else [self.up]
        return [jax.ShapeDtypeStruct(place.lead + block, BF16) for place in places for _ in range(place.count)]

    def pieces(self, arrays, which, rows, spot):
        place = self.down if which else self.up
        arrays = arrays[self.up.count :] if which and self.apart else arrays
        base = rows if which and not self.apart else 0
        extra = () if self.e is None else (self.e,)
        return [(arrays[index], lead + extra, base, b, a) for index, lead, b, a in place.blocks(spot)]


class FfnLoad:
    def __init__(self, place, spot, packs, up, down, sems):
        self.place, self.spot, self.packs, self.up, self.down, self.sems = place, spot, packs, up, down, sems

    def start(self):
        npb, npa = self.place.npb, self.place.npa
        d, ff = self.up.shape
        r, c, dr, dc = d // npb, ff // npa, d // npa, ff // npb
        ups = self.place.pieces(self.packs, 0, r, self.spot)
        downs = self.place.pieces(self.packs, 1, r, self.spot)
        if not self.place.apart:
            downs = sorted(downs, key=lambda piece: piece[3])
            ups = sorted(ups, key=lambda piece: piece[4])
        for k in range(len(ups)):
            array, lead, base, b, a = ups[k]
            pltpu.make_async_copy(array.at[lead + (pl.ds(base, r),)], self.up.at[span(b, r), lane_span(a, c, 0, c)],
                                  self.sems.at[0, a * npb // npa]).start()
            array, lead, base, b, a = downs[k]
            for j in range(dc // c):
                pltpu.make_async_copy(array.at[lead + (pl.ds(base + j * dr, dr),)],
                                      self.down.at[span(a, dr), lane_span(b, dc, j * c, c)], self.sems.at[1, b]).start()

    def wait(self, which, t):
        ref = self.down if which else self.up
        width = ref.shape[1] // self.place.npb
        part = ref.at[:, pl.ds(t * width, width)]
        pltpu.make_async_copy(part, part, self.sems.at[which, t]).wait()


def ffn_fwd_kernel(place, here_ref, spot_ref, *refs):
    packs, refs = refs[: place.count], refs[place.count :]
    (xhat_ref, vec_ref, bup_ref, act_ref, slope_ref, norm_ref, inv_ref, enc_ref, cls_ref, up, down, held, sems) = refs
    step = pl.program_id(0)

    load = FfnLoad(place, here_ref, packs, up, down, sems)

    @pl.when(step == 0)
    def _():
        load.start()

    ff = up.shape[1]
    tiles = bup_ref.shape[0]
    width = ff // tiles
    first_norm = xhat_ref[...] * vec_ref[0:1, :] + vec_ref[1:2, :]
    first_low = first_norm.astype(BF16)
    total = first_norm + vec_ref[7:8, :]
    for t in range(tiles):
        cols = slice(t * width, (t + 1) * width)

        @pl.when(step == 0)
        def _():
            load.wait(0, t)
            load.wait(1, t)

        hidden = mm(first_low, up[:, cols]) + bup_ref[t : t + 1, :]
        cdf = 0.5 + 0.5 * lax.erf(hidden * ROOT_HALF)
        act = (hidden * cdf).astype(BF16)
        act_ref[:, cols] = act
        slope_ref[:, cols] = (cdf + hidden * (jnp.exp(-0.5 * hidden * hidden) * INV_ROOT_TWO_PI)).astype(BF16)
        total = total + mm_nt(act, down[:, cols])
    normed, inverse = norm_rows(total)
    norm_ref[...] = normed
    inv_ref[...] = inverse
    enc = (normed * vec_ref[2:3, :] + vec_ref[3:4, :]).astype(BF16)
    enc_ref[...] = enc
    held[...] = enc.astype(F32)
    for j in range(cls_ref.shape[1]):
        cls_ref[0, j : j + 1, :] = held[pl.ds(spot_ref[step, j], 1), :]


def ffn_fwd(place, here, spots, packs, xhat, vec, bup):
    tokens, d = xhat.shape
    steps, per_row = spots.shape
    ff = bup.shape[0] * bup.shape[1]
    row = lambda width: pl.BlockSpec((FFN_ROW, width), lambda i: (i, 0))
    return pl.pallas_call(
        functools.partial(ffn_fwd_kernel, place),
        grid=(steps,),
        in_specs=[SMEM, SMEM] + [ANY] * place.count + [row(d), whole(vec.shape), whole(bup.shape)],
        out_specs=[row(ff), row(ff), row(d), row(1), row(d), pl.BlockSpec((1, per_row, d), lambda i: (i, 0, 0))],
        out_shape=[
            jax.ShapeDtypeStruct((tokens, ff), BF16),
            jax.ShapeDtypeStruct((tokens, ff), BF16),
            jax.ShapeDtypeStruct((tokens, d), F32),
            jax.ShapeDtypeStruct((tokens, 1), F32),
            jax.ShapeDtypeStruct((tokens, d), BF16),
            jax.ShapeDtypeStruct((steps, per_row, d), F32),
        ],
        scratch_shapes=[pltpu.VMEM((d, ff), BF16), pltpu.VMEM((d, ff), BF16), pltpu.VMEM((FFN_ROW, d), F32),
                        pltpu.SemaphoreType.DMA((2, place.npb))],
        compiler_params=pltpu.CompilerParams(vmem_limit_bytes=58 * MIB),
        cost_estimate=pl.CostEstimate(flops=4 * tokens * d * ff, transcendentals=0, bytes_accessed=40 * MIB),
        name="ffn_fwd",
    )(here, spots, *packs, xhat, vec, bup)


def loss_kernel(scale, q_count, p_count, ids_ref, own_ids_ref, heads_ref, own_ref, loss_ref, gq_ref, gp_ref):
    def split_mm(dot, left, right):
        high = left.astype(BF16)
        rest = left - high.astype(F32)
        mid = rest.astype(BF16)
        tail = (rest - mid.astype(F32)).astype(BF16)
        return dot(high, right) + dot(mid, right) + dot(tail, right)

    def log_norm(scores):
        peak = jnp.max(scores, axis=1, keepdims=True)
        return peak + jnp.log(jnp.sum(jnp.exp(scores - peak), axis=1, keepdims=True))

    def parts(block):
        wide = block.astype(F32)
        d = wide.shape[-1]
        p_rows = wide[:, :p_count].reshape(-1, d).astype(BF16)
        q_rows = wide[:, p_count : p_count + q_count].reshape(-1, d).astype(BF16)
        code = wide[:, p_count + q_count :, :128].reshape(-1, 128)
        return p_rows, q_rows, (code[:, 0:1] * 256.0 + code[:, 1:2]).astype(jnp.int32)

    p_all, q_all, hit_all = parts(heads_ref[...])
    p_own, q_own, hit_own = parts(own_ref[...])
    norm_all = log_norm(mm_nt(q_all, p_all) * scale)
    own_rows = mm_nt(q_own, p_all) * scale
    norm_own = log_norm(own_rows)
    hits = ids_ref[...] == hit_own
    loss_ref[...] = norm_own - jnp.sum(jnp.where(hits, own_rows, 0.0), axis=1, keepdims=True)
    tile = jnp.exp(own_rows - norm_own) - jnp.where(hits, 1.0, 0.0)
    gq_ref[...] = split_mm(mm, tile, p_all) * scale
    own_cols = mm_nt(q_all, p_own) * scale
    hits = own_ids_ref[...] == hit_all
    tile = jnp.exp(own_cols - norm_all) - jnp.where(hits, 1.0, 0.0)
    gp_ref[...] = split_mm(mm_tn, tile, q_all) * scale


def loss_part(ids, own_ids, heads, own, q_count, p_count):
    d = heads.shape[2]
    return pl.pallas_call(
        functools.partial(loss_kernel, 3.0 / math.sqrt(d), q_count, p_count),
        out_shape=[
            jax.ShapeDtypeStruct((q_count, 1), F32),
            jax.ShapeDtypeStruct((q_count, d), F32),
            jax.ShapeDtypeStruct((p_count, d), F32),
        ],
        compiler_params=pltpu.CompilerParams(vmem_limit_bytes=60 * MIB),
        name="loss_part",
    )(ids, own_ids, heads, own)


def ffn_bwd_kernel(place, goal, steps, here_ref, spot_ref, *refs):
    packs, refs = refs[: place.count], refs[place.count :]
    cot_ref, gcls_ref, norm_ref, inv2_ref, act_ref, slope_ref, xhat_ref, inv1_ref, vec_ref, dh_ref = refs[:10]
    grads, refs = refs[10 : 10 + goal.count], refs[10 + goal.count :]
    gvec_ref, gbup_ref, up, down, held, first_t, down_t, hidden_all, act_all, sems = refs
    step = pl.program_id(0)
    tiles = gbup_ref.shape[0]
    ff = up.shape[1]
    width = ff // tiles

    load = FfnLoad(place, here_ref, packs, up, down, sems)

    @pl.when(step == 0)
    def _():
        load.start()
        gvec_ref[...] = jnp.zeros_like(gvec_ref)
        gbup_ref[...] = jnp.zeros_like(gbup_ref)

    @pl.when(step < steps)
    def _():
        held[...] = cot_ref[...].astype(F32)
        for j in range(gcls_ref.shape[1]):
            spot = pl.ds(spot_ref[step, j], 1)
            held[spot, :] = held[spot, :] + gcls_ref[0, j : j + 1, :]
        grad_out = held[...]
        normed = norm_ref[...]
        gvec_ref[2:3, :] += col_sum(grad_out * normed)
        gvec_ref[3:4, :] += col_sum(grad_out)
        grad_two = norm_back(grad_out, vec_ref[2:3, :], normed, inv2_ref[...])
        down_low = grad_two.astype(BF16)
        gvec_ref[7:8, :] += col_sum(down_low.astype(F32))
        tok = pl.ds(pl.multiple_of(step * FFN_ROW, FFN_ROW), FFN_ROW)
        total = grad_two
        for t in range(tiles):
            cols = slice(t * width, (t + 1) * width)

            @pl.when(step == 0)
            def _():
                load.wait(1, t)
                load.wait(0, t)

            hidden = (mm(down_low, down[:, cols]) * slope_ref[:, cols].astype(F32)).astype(BF16)
            hidden_all[tok, cols] = hidden
            gbup_ref[t : t + 1, :] += col_sum(hidden.astype(F32))
            total = total + mm_nt(hidden, up[:, cols])
        act_all[tok, :] = act_ref[...]
        xhat = xhat_ref[...]
        gvec_ref[0:1, :] += col_sum(total * xhat)
        gvec_ref[1:2, :] += col_sum(total)
        dh_ref[...] = norm_back(total, vec_ref[0:1, :], xhat, inv1_ref[...])
        first_low = (xhat * vec_ref[0:1, :] + vec_ref[1:2, :]).astype(BF16)
        for s in range(steps):
            @pl.when(step == s)
            def _():
                first_t[:, s * FFN_ROW : (s + 1) * FFN_ROW] = first_low.T
                down_t[:, s * FFN_ROW : (s + 1) * FFN_ROW] = down_low.T

    npb, npa = goal.npb, goal.npa
    r, c, dr = up.shape[0] // npb, ff // npa, up.shape[0] // npa
    part = ff // npb

    for b in range(npb):
        @pl.when(step == steps + b)
        def _():
            cols = slice(b * part, (b + 1) * part)
            up[:, cols] = mm(first_t[...], hidden_all[:, cols]).astype(BF16)

    @pl.when(step == steps + npb - 1)
    def _():
        for array, lead, base, b, a in goal.pieces(grads, 0, r, here_ref):
            pltpu.make_async_copy(up.at[span(b, r), lane_span(a, c, 0, c)], array.at[lead + (pl.ds(base, r),)],
                                  sems.at[0, 0]).start()

    for b in range(npb):
        @pl.when(step == steps + npb + b)
        def _():
            cols = slice(b * part, (b + 1) * part)
            down[:, cols] = mm(down_t[...], act_all[:, cols]).astype(BF16)

    @pl.when(step == steps + 2 * npb - 1)
    def _():
        for array, lead, base, b, a in goal.pieces(grads, 1, r, here_ref):
            for j in range(part // c):
                pltpu.make_async_copy(down.at[span(a, dr), lane_span(b, part, j * c, c)],
                                      array.at[lead + (pl.ds(base + j * dr, dr),)], sems.at[1, 0]).start()
        pltpu.make_async_copy(up, up, sems.at[0, 0]).wait()
        pltpu.make_async_copy(down, down, sems.at[1, 0]).wait()


def ffn_bwd(place, goal, here, spots, packs, cot, gcls, norm2, inv2, act, slope, xhat, inv1, vec, bup_shape):
    tokens, d = xhat.shape
    steps, per_row = spots.shape
    goal_shapes = goal.shapes(d, act.shape[1])
    ff = act.shape[1]
    last = lambda i: jnp.minimum(i, steps - 1)
    row = lambda width: pl.BlockSpec((FFN_ROW, width), lambda i: (last(i), 0))
    return pl.pallas_call(
        functools.partial(ffn_bwd_kernel, place, goal, steps),
        grid=(steps + 2 * goal.npb,),
        in_specs=[SMEM, SMEM] + [ANY] * place.count + [
            row(d), pl.BlockSpec((1, per_row, d), lambda i: (last(i), 0, 0)), row(d), row(1), row(ff), row(ff), row(d), row(1),
            whole(vec.shape)],
        out_specs=[row(d)] + [ANY] * goal.count + [whole(vec.shape), whole(bup_shape)],
        out_shape=[
            jax.ShapeDtypeStruct((tokens, d), F32),
            *goal_shapes,
            jax.ShapeDtypeStruct(vec.shape, F32),
            jax.ShapeDtypeStruct(bup_shape, F32),
        ],
        scratch_shapes=[pltpu.VMEM((d, ff), BF16), pltpu.VMEM((d, ff), BF16), pltpu.VMEM((FFN_ROW, d), F32),
                        pltpu.VMEM((d, tokens), BF16), pltpu.VMEM((d, tokens), BF16), pltpu.VMEM((tokens, ff), BF16),
                        pltpu.VMEM((tokens, ff), BF16), pltpu.SemaphoreType.DMA((2, place.npb))],
        compiler_params=pltpu.CompilerParams(vmem_limit_bytes=60 * MIB),
        cost_estimate=pl.CostEstimate(flops=8 * tokens * d * ff, transcendentals=0, bytes_accessed=60 * MIB),
        name="ffn_bwd",
    )(here, spots, *packs, cot, gcls, norm2, inv2, act, slope, xhat, inv1, vec)


def attn_bwd_kernel(first, dh_ref, qkv_ref, att_w_ref, segc_ref, segr_ref, gvec_in, proj_in, branch_in, proj, branch, gvec):
    d = dh_ref.shape[1]

    @pl.when(pl.program_id(0) == 0)
    def _():
        gvec[...] = gvec_in[...]

    low = dh_ref[...].astype(BF16)
    branch[...] = low
    gvec[6:7, :] += col_sum(low.astype(F32))
    att_grad = mm_nt(low, att_w_ref[...]).astype(BF16)
    blocked = jnp.where(segc_ref[0][:, 1:2] == segr_ref[0][0:1, :], 0.0, NEG_FILL)
    low_half = lax.broadcasted_iota(jnp.int32, (1, 2 * HD), 1) < HD
    keep = (low_half.astype(F32).astype(BF16), (1.0 - low_half.astype(F32)).astype(BF16))
    for p in range(d // (2 * HD)):
        lanes = slice(p * 2 * HD, (p + 1) * 2 * HD)
        k_lanes = slice(d + p * 2 * HD, d + (p + 1) * 2 * HD)
        v_lanes = slice(2 * d + p * 2 * HD, 2 * d + (p + 1) * 2 * HD)
        q2 = qkv_ref[:, lanes]
        k2 = qkv_ref[:, k_lanes]
        v2 = qkv_ref[:, v_lanes]
        g2 = att_grad[:, lanes]
        dq, dk, dv = [], [], []
        for h in range(2):
            scores = mm_nt(k2 * keep[h], q2) + blocked
            terms = jnp.exp(scores - jnp.max(scores, axis=0, keepdims=True))
            prob = terms * (1.0 / jnp.sum(terms, axis=0, keepdims=True))
            weighed = prob * mm_nt(v2 * keep[h], g2)
            sgrad = (weighed - prob * jnp.sum(weighed, axis=0, keepdims=True)).astype(BF16)
            dv.append(mm(prob.astype(BF16), g2))
            dk.append(mm(sgrad, q2))
            dq.append(mm_tn(sgrad, k2))
        proj[:, lanes] = (jnp.where(low_half, dq[0], dq[1]) * (HD ** -0.5)).astype(BF16)
        proj[:, k_lanes] = jnp.where(low_half, dk[0], dk[1]).astype(BF16)
        proj[:, v_lanes] = jnp.where(low_half, dv[0], dv[1]).astype(BF16)
    gvec[4:5, :] += col_sum(proj[:, :d].astype(F32))
    gvec[5:6, :] += col_sum(proj[:, 2 * d :].astype(F32))


def attn_bwd(first, last, dh, qkv, segc, segr, wout, gvec, before):
    tokens, d = dh.shape
    row = lambda width: pl.BlockSpec((ROW, width), lambda i: (i + first, 0))
    shapes = [jax.ShapeDtypeStruct((tokens, 3 * d), BF16), jax.ShapeDtypeStruct((tokens, d), BF16)]
    if before is None:
        kernel = lambda *refs: attn_bwd_kernel(first, *refs[:6], None, None, *refs[6:])
    else:
        kernel = lambda *refs: attn_bwd_kernel(first, *refs)
    return pl.pallas_call(
        kernel,
        grid=(last - first,),
        in_specs=[row(d), row(3 * d), whole(wout.shape), pl.BlockSpec((1, ROW, 2), lambda i: (i + first, 0, 0)),
                  pl.BlockSpec((1, 2, ROW), lambda i: (i + first, 0, 0)), whole(gvec.shape)]
        + ([] if before is None else [ANY, ANY]),
        out_specs=[row(3 * d), row(d), whole(gvec.shape)],
        out_shape=shapes + [jax.ShapeDtypeStruct(gvec.shape, F32)],
        input_output_aliases={} if before is None else {6: 0, 7: 1},
        compiler_params=pltpu.CompilerParams(vmem_limit_bytes=60 * MIB),
        cost_estimate=pl.CostEstimate(flops=(last - first) * ROW * d * (2 * d + 40 * ROW), transcendentals=0,
                                      bytes_accessed=8 * MIB),
        name="attn_bwd",
    )(dh, qkv, wout, segc, segr, gvec, *(before or ()))


def attn_grad_kernel(dims, goals, here_ref, x_ref, att_ref, proj_ref, branch_ref, gvec, gbup, *refs):
    total = sum(goal.count for goal, _, _ in goals)
    grads, (x_t, wide, out, main, extra, sems) = refs[:total], refs[total:]
    npb, npa, r, wq, wo, rows_per, w1, w2 = dims
    step = pl.program_id(0)
    d = x_ref.shape[1]
    c = wq + wo

    def widen(piece):
        if piece.shape[1] == c:
            return piece
        return jnp.concatenate([piece, jnp.zeros((piece.shape[0], c - piece.shape[1]), F32)], axis=1)

    def multiply(g):
        wide[:, g * d : (g + 1) * d] = mm(x_t[...], proj_ref[...]).astype(BF16)

    def fill(g):
        for a in range(npa):
            if -(-(a + 1) * wq // d) == g:
                main[a] = jnp.concatenate([wide[:, a * wq : (a + 1) * wq], out[:, a * wo : (a + 1) * wo]], axis=1)

    @pl.when(step == 0)
    def _():
        x_t[...] = x_ref[...].T
        multiply(0)
        out[...] = mm(att_ref[...].T, branch_ref[...]).astype(BF16)

    for g in range(1, 3):
        @pl.when(step == g)
        def _():
            multiply(g)
            fill(g)

    @pl.when(step == 3)
    def _():
        fill(3)
        for b in range(npb):
            for a in range(npa):
                rows = [widen(gvec[b * rows_per : (b + 1) * rows_per, a * w1 : (a + 1) * w1]),
                        widen(gbup[b : b + 1, a * w2 : (a + 1) * w2]),
                        jnp.zeros((EXTRA - 1 - rows_per, c), F32)]
                extra[b * npa + a] = jnp.concatenate(rows, axis=0).astype(BF16)
        base = 0
        for goal, low, high in goals:
            top = min(high, r)
            for index, lead, b, a in goal.blocks(here_ref):
                target = grads[base + index]
                start = b * r + low
                if not isinstance(start, int):
                    start = pl.multiple_of(start, 16)
                pltpu.make_async_copy(main.at[a, pl.ds(start, top - low)], target.at[lead + (pl.ds(0, top - low),)],
                                      sems.at[0]).start()
                if high > r:
                    pltpu.make_async_copy(extra.at[b * npa + a], target.at[lead + (pl.ds(r - low, EXTRA),)],
                                          sems.at[1]).start()
            base += goal.count
        pltpu.make_async_copy(main, main, sems.at[0]).wait()
        pltpu.make_async_copy(extra, extra, sems.at[1]).wait()


def attn_grad(dims, goals, here, x, att, proj, branch, gvec, gbup):
    npb, npa, r, wq, wo, rows_per, w1, w2 = dims
    tokens, d = x.shape
    c = wq + wo
    return pl.pallas_call(
        functools.partial(attn_grad_kernel, dims, goals),
        grid=(4,),
        in_specs=[SMEM, whole(x.shape), whole(att.shape), pl.BlockSpec((tokens, d), lambda i: (0, jnp.minimum(i, 2))),
                  whole(branch.shape), whole(gvec.shape), whole(gbup.shape)],
        out_specs=[ANY] * sum(goal.count for goal, _, _ in goals),
        out_shape=[jax.ShapeDtypeStruct(goal.lead + (high - low, c), BF16)
                   for goal, low, high in goals for _ in range(goal.count)],
        scratch_shapes=[pltpu.VMEM((d, tokens), BF16), pltpu.VMEM((d, 3 * d), BF16), pltpu.VMEM((d, d), BF16),
                        pltpu.VMEM((npa, d, c), BF16),
                        pltpu.VMEM((npb * npa, EXTRA, c), BF16), pltpu.SemaphoreType.DMA((2,))],
        compiler_params=pltpu.CompilerParams(vmem_limit_bytes=60 * MIB),
        cost_estimate=pl.CostEstimate(flops=8 * tokens * d * d, transcendentals=0, bytes_accessed=16 * MIB),
        name="attn_grad",
    )(here, x, att, proj, branch, gvec, gbup)


def input_grad_kernel(proj_ref, weight_ref, dh_ref, out_ref):
    out_ref[...] = mm_nt(proj_ref[...], weight_ref[...]) + dh_ref[...]


def input_grad(proj, wqkv, dh):
    tokens, d = dh.shape
    row = lambda width: pl.BlockSpec((ROW, width), lambda i: (i, 0))
    return pl.pallas_call(
        input_grad_kernel,
        grid=(tokens // ROW,),
        in_specs=[row(3 * d), whole(wqkv.shape), row(d)],
        out_specs=row(d),
        out_shape=jax.ShapeDtypeStruct((tokens, d), F32),
        compiler_params=pltpu.CompilerParams(vmem_limit_bytes=60 * MIB),
        cost_estimate=pl.CostEstimate(flops=6 * tokens * d * d, transcendentals=0, bytes_accessed=16 * MIB),
        name="input_grad",
    )(proj, wqkv, dh)


class Blocks:
    def __init__(self, npb, npa, d, ff):
        self.npb, self.npa, self.d, self.ff = npb, npa, d, ff
        self.r, self.wq, self.wo, self.c = d // npb, 3 * d // npa, d // npa, ff // npa
        self.dr, self.dc = d // npa, ff // npb
        self.rows_per, self.w1, self.w2 = 8 // npb, d // npa, ff // (npa * npb)
        self.direct = self.c % 128 == 0 and self.r % 16 == 0 and self.dr % 16 == 0
        if self.direct:
            self.dims = (npb, npa, self.r, self.wq, self.wo, self.rows_per, self.w1, self.w2)
        else:
            self.dims = (1, 1, d, 3 * d, d, 8, d, ff)

    def pack(self, w_qkv, w_out, w_up, w_down, norm_bias, bias_up):
        c = self.wq + self.wo
        vec = jnp.pad(norm_bias, ((0, 0), (0, 0), (0, c - self.w1)))
        bup = jnp.pad(bias_up[:, None, :], ((0, 0), (0, EXTRA - 1 - self.rows_per), (0, c - self.w2)))
        attn = jnp.concatenate([jnp.concatenate([w_qkv, w_out], axis=2), vec, bup], axis=1)
        down_t = jnp.swapaxes(w_down, 1, 2)
        down = jnp.concatenate([down_t[:, :, j : j + self.c] for j in range(0, self.dc, self.c)], axis=1)
        return attn, jnp.concatenate([w_up, down], axis=1)

    def from_blocks(self, attn, ffn):
        if self.direct:
            return attn, ffn
        d, ff, r = self.d, self.ff, self.r
        rows = lambda part, height: part.transpose(0, 2, 1, 3).reshape(height, -1)
        qkv = rows(attn[:, :, :r, : self.wq], d)
        out = rows(attn[:, :, :r, self.wq :], d)
        vec = rows(attn[:, :, r : r + self.rows_per, : self.w1], 8)
        bup = attn[:, :, r + self.rows_per, : self.w2].reshape(1, ff)
        vec = jnp.pad(vec, ((0, 0), (0, 3 * d)))
        bup = jnp.pad(bup, ((0, EXTRA - 9), (0, 4 * d - ff)))
        wide = jnp.concatenate([jnp.concatenate([qkv, out], axis=1), vec, bup], axis=0)
        up = rows(ffn[:, :, :r], d)
        pieces = self.dc // self.c
        down = ffn[:, :, r:].reshape(self.npb, self.npa, pieces, self.dr, self.c)
        down = down.transpose(1, 3, 0, 2, 4).reshape(d, ff)
        return wide[None, None], jnp.concatenate([up, down])[None, None]

    def to_blocks(self, attn, ffn):
        if self.direct:
            return attn, ffn
        d, ff, npb, npa = self.d, self.ff, self.npb, self.npa
        blocks = lambda part, height: part.reshape(npb, height, npa, -1).transpose(0, 2, 1, 3)
        wide = attn[0, 0]
        c = self.wq + self.wo
        main = jnp.concatenate([blocks(wide[:d, : 3 * d], self.r), blocks(wide[:d, 3 * d :], self.r)], axis=3)
        vec = blocks(wide[d : d + 8, :d], self.rows_per)
        vec = jnp.pad(vec, ((0, 0), (0, 0), (0, 0), (0, c - self.w1)))
        bup = wide[d + 8, :ff].reshape(npb, npa, 1, self.w2)
        bup = jnp.pad(bup, ((0, 0), (0, 0), (0, EXTRA - 1 - self.rows_per), (0, c - self.w2)))
        pieces = self.dc // self.c
        down = ffn[0, 0, d:].reshape(npa, self.dr, npb, pieces, self.c).transpose(2, 0, 3, 1, 4)
        down = down.reshape(npb, npa, pieces * self.dr, self.c)
        return jnp.concatenate([main, vec, bup], axis=2), jnp.concatenate([blocks(ffn[0, 0, :d], self.r), down], axis=2)

    def unpack(self, attn, ffn):
        r = self.r
        attn, ffn = jnp.stack(attn), jnp.stack(ffn)
        down = ffn[:, r:]
        down = jnp.concatenate([down[:, j * self.dr : (j + 1) * self.dr] for j in range(self.dc // self.c)], axis=2)
        return (attn[:, :r, : self.wq], attn[:, :r, self.wq :], ffn[:, :r], jnp.swapaxes(down, 1, 2),
                attn[:, r : r + self.rows_per, : self.w1], attn[:, r + self.rows_per, : self.w2])


BOTH = ("pb", "pa")
BITS = {"core": 8, "y": 16, "z1": 2, "z2": 4, "z3": 6, "x": 1, "xy": 17}


def swap(block, way):
    return lax.ppermute(block, BOTH, [(i, i ^ BITS[way]) for i in range(32)])


class Gather:
    def __init__(self, block, ways):
        self.held, self.ways = [block], ways

    def after(self, *others):
        late = [held for other in others for held in other.held]
        self.held = list(lax.optimization_barrier((tuple(self.held), tuple(late)))[0])

    def step(self, stage):
        if stage == 0:
            block = self.held[0]
            self.held = [jnp.stack([block] + [swap(block, way) for way in ("z1", "z2", "z3")])]
        else:
            way = self.ways[stage - 1] if stage < 3 else "core"
            self.held = self.held + [swap(part, way) for part in self.held]


def gather_heads(block):
    near = jnp.stack([block] + [swap(block, way) for way in ("z1", "z2", "z3")])
    wide = jnp.stack([near] + [swap(near, way) for way in ("x", "y", "xy")])
    return jnp.stack([wide, swap(wide, "core")]).reshape((-1,) + block.shape)


HEAD_ORDER = [c ^ s ^ z for c in (0, 8) for s in (0, 1, 16, 17) for z in (0, 2, 4, 6)]


class Scatter:
    def __init__(self, keep, send, ways):
        self.terms, self.ways = [(keep, ()), (send, ())], ways

    def newest(self, line, count):
        arrays, spots = zip(*self.terms)
        fresh = line.wait(arrays[-count:])
        self.terms = list(zip(arrays[:-count] + tuple(fresh), spots))

    def sum(self, *pick):
        return sum(array[spot + pick].astype(F32) for array, spot in self.terms)

    def step(self, stage, line):
        if stage == 0:
            self.terms = [self.terms[0], (swap(self.terms[1][0], "core"), ())]
            return
        self.newest(line, 1)
        ways = (self.ways[stage - 1],) if stage < 3 else ("z1", "z2", "z3")
        parts = [self.sum(j).astype(BF16) for j in range(1, len(ways) + 1)]
        line.mark(parts)
        self.terms = [(array, spot + (0,)) for array, spot in self.terms] + [
            (swap(part, way), ()) for part, way in zip(parts, ways)]

    def total(self, line):
        self.newest(line, 3)
        return line.mark(self.sum())


class Line:
    def __init__(self):
        self.last = None

    def wait(self, operands):
        if self.last is None:
            return operands
        return lax.optimization_barrier((operands, self.last))[0]

    def mark(self, result):
        self.last = jax.tree.leaves(result)[0]
        return result

    def run(self, step, *operands):
        return self.mark(step(*self.wait(operands)))


def body(questions, passages, cot_questions, cot_passages, question_lengths, segment_lengths, positives, w_qkv, w_out, w_up,
         w_down, norm_bias, bias_up):
    q_count, q_len, d = questions.shape
    row_count, row_len, _ = passages.shape
    segs = segment_lengths.shape[1]
    npb, npa = lax.axis_size("pb"), lax.axis_size("pa")
    size = Blocks(npb, npa, d, bias_up.shape[1] * npb * npa)
    dims = size.dims
    near = size.direct and (npb, npa) == (4, 8)
    pb, pa = lax.axis_index("pb"), lax.axis_index("pa")
    device = pb * npa + pa
    here = jnp.stack([pb // 2, pb % 2, pa // 2, pa % 2]).astype(jnp.int32)
    order = (("y", "x"), ("x", "y"))

    attn_pack, ffn_pack = size.pack(w_qkv, w_out, w_up, w_down, norm_bias, bias_up)
    mesh_order = Place(dims[0], dims[1], None, False)
    one_array = FfnPlace(mesh_order)
    if near:
        ffn_all = lax.all_gather(ffn_pack, BOTH, axis=0).reshape((npb, npa) + ffn_pack.shape)
        parts = [Gather(attn_pack[e], order[e]) for e in range(2)]
        for stage in range(4):
            for each in parts:
                each.step(stage)
        attn_w = [each.held for each in parts]
        attn_into = [Place(npb, npa, order[e][0], True) for e in range(2)]
        ffn_w = [[ffn_all]] * 2
        ffn_into = [FfnPlace(mesh_order, e=e) for e in range(2)]
    else:
        attn_all = lax.all_gather(attn_pack, BOTH, axis=0).reshape((npb, npa) + attn_pack.shape)
        ffn_all = lax.all_gather(ffn_pack, BOTH, axis=0).reshape((npb, npa) + ffn_pack.shape)
        attn_w, ffn_w = zip(*[size.from_blocks(attn_all[:, :, e], ffn_all[:, :, e]) for e in range(2)])
        attn_w = [[blocks] for blocks in attn_w]
        ffn_w = [[blocks] for blocks in ffn_w]
        attn_into = [mesh_order] * 2
        ffn_into = [one_array] * 2

    per_row = ROW // q_len
    q_rows = q_count // per_row
    token = jnp.arange(ROW, dtype=jnp.int32)
    q_seg = jnp.broadcast_to(token // q_len, (q_rows, ROW))
    q_valid = (token % q_len)[None, :] < jnp.repeat(question_lengths.reshape(q_rows, per_row), q_len, axis=1)
    starts = jnp.cumsum(segment_lengths, axis=1) - segment_lengths
    p_seg = jnp.sum((token[None, None, :] >= starts[:, :, None]).astype(jnp.int32), axis=1)
    segr = (jnp.stack([q_seg, jnp.where(q_valid, q_seg, -1)], axis=1), jnp.stack([p_seg, p_seg], axis=1))
    segc = tuple(jnp.swapaxes(pair, 1, 2) for pair in segr)
    spots = (jnp.broadcast_to(jnp.arange(per_row, dtype=jnp.int32) * q_len, (q_rows, per_row)), starts)
    xs = (questions.reshape(-1, d), passages.reshape(-1, d))
    cots = [cot_questions.reshape(-1, d), cot_passages.reshape(-1, d)]
    p_count = row_count * segs

    def by_step(spots):
        rows = FFN_ROW // ROW
        base = jnp.arange(spots.shape[0], dtype=jnp.int32) % rows * ROW
        return (spots + base[:, None]).reshape(-1, rows * spots.shape[1])

    spots = tuple(by_step(each) for each in spots)
    own_hits = lax.dynamic_slice_in_dim(positives, pa * q_count, q_count)
    code = jnp.pad(jnp.stack([own_hits // 256, own_hits % 256], axis=1).astype(BF16), ((0, 0), (0, d - 2)))
    listed = device ^ jnp.array(HEAD_ORDER, jnp.int32) if near else jnp.arange(npb * npa, dtype=jnp.int32)
    ids = (listed[:, None] * p_count + jnp.arange(p_count, dtype=jnp.int32)[None, :]).reshape(1, -1)
    own_ids = device * p_count + jnp.arange(p_count, dtype=jnp.int32)[None, :]

    line = Line()
    half = [
        line.run(lambda x, *packs, e=e: attn_fwd(dims, attn_into[e], here, packs, x, segc[e], segr[e]), xs[e], *attn_w[e])
        for e in range(2)
    ]
    done = [None, None]
    for e in (0, 1):
        done[e] = line.run(
            lambda *packs, e=e: ffn_fwd(ffn_into[e], here, spots[e], packs, half[e][2], half[e][6], half[e][7]), *ffn_w[e])
    own = jnp.concatenate([done[1][5].reshape(p_count, d).astype(BF16), done[0][5].reshape(q_count, d).astype(BF16), code])
    heads = gather_heads(own) if near else lax.all_gather(own, BOTH, axis=0)
    losses, gq, gp = loss_part(ids, own_ids, heads, own[None], q_count, p_count)
    gcls = tuple(grad.reshape(each.shape + (d,)) for grad, each in zip((gq, gp), spots))

    def ffn_step(e, goal, cot):
        _, _, xhat, inv1, _, _, vec, bup = half[e]
        act, slope, norm2, inv2, _, _ = done[e]
        dh, *blocks, gvec, gbup = ffn_bwd(ffn_into[e], goal, here, spots[e], ffn_w[e], cot, gcls[e], norm2,
                                          inv2, act, slope, xhat, inv1, vec, bup.shape)
        return dh, blocks, gvec, gbup

    def attn_rows(e, first, last, dh, gvec, before):
        return attn_bwd(first, last, dh, half[e][0], segc[e], segr[e], half[e][5], gvec, before)

    def attn_weights(e, goals, rows, gbup):
        return attn_grad(dims, goals, here, xs[e], half[e][1], rows[0], rows[1], rows[2], gbup)

    def scatter(blocks):
        flat = blocks.reshape((npb * npa,) + blocks.shape[2:])
        return lax.psum_scatter(flat, BOTH, scatter_dimension=0, tiled=False).astype(F32)

    counts = (q_rows, row_count)
    if near:
        whole_block = attn_pack.shape[1]
        cut = whole_block // 32 * 16 + 16
        out_place = {way[0]: Place(npb, npa, way[0], False) for way in order}
        line = Line()
        dh_q, blocks_q, gvec_q, gbup_q = line.run(lambda cot: ffn_step(0, one_array, cot), cots[0])
        sum_q = scatter(blocks_q[0])
        dh_p, blocks_p, gvec_p, gbup_p = line.run(lambda cot: ffn_step(1, FfnPlace(out_place["y"]), cot), cots[1])
        ffn_p = Scatter(*blocks_p, order[0])
        ffn_p.step(0, line)

        rows_q = line.run(lambda dh: attn_rows(0, 0, q_rows, dh, gvec_q, None), dh_q)
        ffn_p.step(1, line)
        got = line.run(lambda *rows: attn_weights(0, [(out_place["x"], 0, whole_block)], rows, gbup_q), *rows_q)
        attn_q = Scatter(*got, order[1])
        attn_q.step(0, line)
        middle = row_count // 2
        rows_p = line.run(lambda dh: attn_rows(1, 0, middle, dh, gvec_p, None), dh_p)
        attn_q.step(1, line)
        rows_p = line.run(lambda *rows: attn_rows(1, middle, row_count, dh_p, rows[2], rows[:2]), *rows_p)
        goals = [(out_place["y"], 0, cut), (out_place["x"], cut, whole_block)]
        got = line.run(lambda *rows: attn_weights(1, goals, rows, gbup_p), *rows_p)
        attn_p = [Scatter(*got[:2], order[0]), Scatter(*got[2:], order[1])]
        for each in attn_p:
            each.step(0, line)
        ffn_p.step(2, line)
        attn_q.step(2, line)
        gx_q = line.run(lambda proj: input_grad(proj, half[0][4], dh_q), rows_q[0])
        for each in attn_p:
            each.step(1, line)
        gx_p = line.run(lambda proj: input_grad(proj, half[1][4], dh_p), rows_p[0])
        gx = (gx_q, gx_p)
        ffn_p.step(3, line)
        attn_q.step(3, line)
        for stage in (2, 3):
            for each in attn_p:
                each.step(stage, line)
        sums = [each.total(line) for each in [ffn_p, attn_q] + attn_p]
        ffn_sum = [sum_q, sums[0]]
        attn_sum = [sums[1], jnp.concatenate(sums[2:])]
    else:
        pairs, gx = [], []
        for e in range(2):
            dh, blocks, gvec, gbup = ffn_step(e, one_array, cots[e])
            rows = attn_rows(e, 0, counts[e], dh, gvec, None)
            got = attn_weights(e, [(mesh_order, 0, dims[2] + EXTRA)], rows, gbup)
            pairs.append(size.to_blocks(got[0], blocks[0]))
            gx.append(input_grad(rows[0], half[e][4], dh))
        attn_sum = [scatter(pair[0]) for pair in pairs]
        ffn_sum = [scatter(pair[1]) for pair in pairs]
    outs = size.unpack(attn_sum, ffn_sum)
    return (
        done[0][4].reshape(questions.shape),
        done[1][4].reshape(passages.shape),
        losses[:, 0],
        gx[0].reshape(questions.shape),
        gx[1].reshape(passages.shape),
    ) + outs


def solution(mesh):
    rows = P(BOTH, None, None)
    shard = P(None, "pb", "pa")
    vector = P(None, BOTH)
    in_specs = (rows, rows, rows, rows, P(BOTH), P(BOTH, None), P("pb"), shard, shard, shard, shard, shard, vector)
    out_specs = (rows, rows, P(BOTH), rows, rows, shard, shard, shard, shard, shard, vector)
    return jax.shard_map(body, mesh=mesh, in_specs=in_specs, out_specs=out_specs, check_vma=False)
```

```python
import functools
import math

import jax
import jax.numpy as jnp
from jax import lax
from jax.experimental import pallas as pl
from jax.experimental.pallas import tpu as pltpu
from jax.sharding import PartitionSpec as P

HD = 64
EXTRA = 16
ROW = 256
FFN_ROW = 256
NEG_FILL = -1000000000.0
EPSILON = 1e-06
ROOT_HALF = 0.7071067811865476
INV_ROOT_TWO_PI = 0.3989422804014327
F32 = jnp.float32
BF16 = jnp.bfloat16
MIB = 1 << 20
ANY = pl.BlockSpec(memory_space=pl.ANY)
SMEM = pl.BlockSpec(memory_space=pltpu.SMEM)
BRIEF = pl.CostEstimate(flops=1, transcendentals=0, bytes_accessed=1)


def mm(left, right):
    return lax.dot_general(left, right, (((1,), (0,)), ((), ())), preferred_element_type=F32)


def mm_nt(left, right):
    return lax.dot_general(left, right, (((1,), (1,)), ((), ())), preferred_element_type=F32)


def mm_tn(left, right):
    return lax.dot_general(left, right, (((0,), (0,)), ((), ())), preferred_element_type=F32)


def whole(shape):
    return pl.BlockSpec(shape, lambda i: (0,) * len(shape), pipeline_mode=pl.Buffered(1))


def norm_rows(summed):
    centred = summed - jnp.mean(summed, axis=-1, keepdims=True)
    inverse = lax.rsqrt(jnp.mean(centred * centred, axis=-1, keepdims=True) + EPSILON)
    return centred * inverse, inverse


def norm_back(grad_out, gain, normed, inverse):
    scaled = grad_out * gain
    inner = (
        scaled
        - jnp.mean(scaled, axis=-1, keepdims=True)
        - normed * jnp.mean(scaled * normed, axis=-1, keepdims=True)
    )
    return inverse * inner


def col_sum(block):
    return jnp.sum(block, axis=0, keepdims=True)


class Place:
    def __init__(self, npb, npa, first, into):
        self.npb, self.npa, self.first, self.into = npb, npa, first, into
        self.count = 1 if first is None else 8 if into else 2
        self.lead = (npb, npa) if first is None else (4,) if into else (2, 2, 4)

    def blocks(self, spot):
        if self.first is None:
            return [(0, (b, a), b, a) for b in range(self.npb) for a in range(self.npa)]
        y, core, z, x = (spot[k] for k in range(4))
        found = []
        for core_d in range(2):
            for second in range(2):
                for first in range(2):
                    for z_d in range(4):
                        y_d, x_d = (first, second) if self.first == "y" else (second, first)
                        index = core_d * 4 + second * 2 + first if self.into else core_d
                        lead = (z_d,) if self.into else (first, second, z_d)
                        b = lax.bitwise_xor(y, y_d) * 2 + lax.bitwise_xor(core, core_d)
                        a = lax.bitwise_xor(z, z_d) * 2 + lax.bitwise_xor(x, x_d)
                        found.append((index, lead, b, a))
        return found


def span(index, length):
    start = index * length
    if isinstance(start, int):
        return pl.ds(start, length)
    return pl.ds(pl.multiple_of(start, math.gcd(length, 1 << 20)), length)


def lane_span(index, stride, base, length):
    start = index * stride + base
    if isinstance(start, int):
        return pl.ds(start, length)
    return pl.ds(pl.multiple_of(start, 128), length)


def attn_fwd_kernel(dims, place, here_ref, *refs):
    packs, refs = refs[: place.count], refs[place.count :]
    (x_ref, segc_ref, segr_ref, qkv_ref, att_ref, xhat_ref, inv_ref, wqkv_ref, wout_ref, vec_ref, bup_ref, held, sem) = refs
    npb, npa, r, wq, wo, rows_per, w1, w2 = dims
    d = x_ref.shape[1]

    @pl.when(pl.program_id(0) == 0)
    def _():
        for index, lead, b, a in place.blocks(here_ref):
            pltpu.make_async_copy(packs[index].at[lead], held.at[b, a], sem).start()
        pltpu.make_async_copy(held, held, sem).wait()
        for b in range(npb):
            rows = pl.ds(b * r, r)
            wqkv_ref[rows, :] = jnp.concatenate([held[b, a, :r, :wq] for a in range(npa)], axis=1)
            wout_ref[rows, :] = jnp.concatenate([held[b, a, :r, wq:] for a in range(npa)], axis=1)
            extra = [held[b, a, r:, :].astype(F32) for a in range(npa)]
            vec_ref[pl.ds(b * rows_per, rows_per), :] = jnp.concatenate(
                [part[:rows_per, :w1] for part in extra], axis=1)
            bup_ref[b : b + 1, :] = jnp.concatenate(
                [part[rows_per : rows_per + 1, :w2] for part in extra], axis=1)

    flat = x_ref[...]
    qkv_ref[:, :d] = ((mm(flat, wqkv_ref[:, :d]) + vec_ref[4:5, :]).astype(BF16) * BF16(HD ** -0.5))
    qkv_ref[:, d : 2 * d] = mm(flat, wqkv_ref[:, d : 2 * d]).astype(BF16)
    qkv_ref[:, 2 * d :] = (mm(flat, wqkv_ref[:, 2 * d :]) + vec_ref[5:6, :]).astype(BF16)
    blocked = jnp.where(segc_ref[0][:, 0:1] == segr_ref[0][1:2, :], 0.0, NEG_FILL)
    low_half = lax.broadcasted_iota(jnp.int32, (1, 2 * HD), 1) < HD
    keep = (low_half.astype(F32).astype(BF16), (1.0 - low_half.astype(F32)).astype(BF16))
    for p in range(d // (2 * HD)):
        lanes = slice(p * 2 * HD, (p + 1) * 2 * HD)
        q2 = qkv_ref[:, lanes]
        k2 = qkv_ref[:, d + p * 2 * HD : d + (p + 1) * 2 * HD]
        v2 = qkv_ref[:, 2 * d + p * 2 * HD : 2 * d + (p + 1) * 2 * HD]
        parts = []
        for h in range(2):
            scores = mm_nt(q2 * keep[h], k2) + blocked
            terms = jnp.exp(scores - jnp.max(scores, axis=-1, keepdims=True))
            total = jnp.sum(terms, axis=-1, keepdims=True)
            prob = (terms * (1.0 / total)).astype(BF16)
            parts.append(mm(prob, v2))
        att_ref[:, lanes] = jnp.where(low_half, parts[0], parts[1]).astype(BF16)
    branch = mm(att_ref[...], wout_ref[...]) + vec_ref[6:7, :]
    normed, inverse = norm_rows(flat.astype(F32) + branch)
    xhat_ref[...] = normed
    inv_ref[...] = inverse


def attn_fwd(dims, place, here, packs, x, segc, segr):
    npb, npa, r, wq, wo, rows_per, w1, w2 = dims
    tokens, d = x.shape
    steps = tokens // ROW
    ff = w2 * npa * npb
    row = lambda width: pl.BlockSpec((ROW, width), lambda i: (i, 0))
    return pl.pallas_call(
        functools.partial(attn_fwd_kernel, dims, place),
        grid=(steps,),
        in_specs=[SMEM] + [ANY] * place.count + [row(d), pl.BlockSpec((1, ROW, 2), lambda i: (i, 0, 0)),
                  pl.BlockSpec((1, 2, ROW), lambda i: (i, 0, 0))],
        out_specs=[row(3 * d), row(d), row(d), row(1), whole((d, 3 * d)), whole((d, d)), whole((8, d)),
                   whole((npb, ff // npb))],
        out_shape=[
            jax.ShapeDtypeStruct((tokens, 3 * d), BF16),
            jax.ShapeDtypeStruct((tokens, d), BF16),
            jax.ShapeDtypeStruct((tokens, d), F32),
            jax.ShapeDtypeStruct((tokens, 1), F32),
            jax.ShapeDtypeStruct((d, 3 * d), BF16),
            jax.ShapeDtypeStruct((d, d), BF16),
            jax.ShapeDtypeStruct((8, d), F32),
            jax.ShapeDtypeStruct((npb, ff // npb), F32),
        ],
        scratch_shapes=[pltpu.VMEM((npb, npa, r + EXTRA, wq + wo), BF16), pltpu.SemaphoreType.DMA],
        compiler_params=pltpu.CompilerParams(vmem_limit_bytes=58 * MIB),
        cost_estimate=BRIEF,
        name="attn_fwd",
    )(here, *packs, x, segc, segr)


class FfnPlace:
    def __init__(self, up, down=None, e=None):
        self.up, self.down, self.e = up, down or up, e
        self.npb, self.npa, self.count = up.npb, up.npa, up.count

    def shapes(self, d, ff):
        block = (d // self.npb * 2, ff // self.npa)
        return [jax.ShapeDtypeStruct(self.up.lead + block, BF16)] * self.count

    def pieces(self, arrays, which, rows, spot):
        place = self.down if which else self.up
        extra = () if self.e is None else (self.e,)
        return [(arrays[index], lead + extra, rows if which else 0, b, a) for index, lead, b, a in place.blocks(spot)]


class FfnLoad:
    def __init__(self, place, spot, packs, up, down, sems):
        self.place, self.spot, self.packs, self.up, self.down, self.sems = place, spot, packs, up, down, sems

    def start(self):
        npb, npa = self.place.npb, self.place.npa
        d, ff = self.up.shape
        r, c, dr, dc = d // npb, ff // npa, d // npa, ff // npb
        ups = self.place.pieces(self.packs, 0, r, self.spot)
        downs = self.place.pieces(self.packs, 1, r, self.spot)
        if self.place.up.first is None:
            downs = sorted(downs, key=lambda piece: piece[3])
            ups = sorted(ups, key=lambda piece: piece[4])
        for k in range(len(ups)):
            array, lead, base, b, a = ups[k]
            pltpu.make_async_copy(array.at[lead + (pl.ds(base, r),)], self.up.at[span(b, r), lane_span(a, c, 0, c)],
                                  self.sems.at[0, a * npb // npa]).start()
            array, lead, base, b, a = downs[k]
            for j in range(dc // c):
                pltpu.make_async_copy(array.at[lead + (pl.ds(base + j * dr, dr),)],
                                      self.down.at[span(a, dr), lane_span(b, dc, j * c, c)], self.sems.at[1, b]).start()

    def wait(self, which, t):
        ref = self.down if which else self.up
        width = ref.shape[1] // self.place.npb
        part = ref.at[:, pl.ds(t * width, width)]
        pltpu.make_async_copy(part, part, self.sems.at[which, t]).wait()


def ffn_fwd_kernel(place, here_ref, spot_ref, *refs):
    packs, refs = refs[: place.count], refs[place.count :]
    (xhat_ref, vec_ref, bup_ref, act_ref, slope_ref, norm_ref, inv_ref, enc_ref, cls_ref, up, down, held, sems) = refs
    step = pl.program_id(0)

    load = FfnLoad(place, here_ref, packs, up, down, sems)

    @pl.when(step == 0)
    def _():
        load.start()

    ff = up.shape[1]
    tiles = bup_ref.shape[0]
    width = ff // tiles
    first_norm = xhat_ref[...] * vec_ref[0:1, :] + vec_ref[1:2, :]
    first_low = first_norm.astype(BF16)
    total = first_norm + vec_ref[7:8, :]
    for t in range(tiles):
        cols = slice(t * width, (t + 1) * width)

        @pl.when(step == 0)
        def _():
            load.wait(0, t)
            load.wait(1, t)

        hidden = mm(first_low, up[:, cols]) + bup_ref[t : t + 1, :]
        cdf = 0.5 + 0.5 * lax.erf(hidden * ROOT_HALF)
        act = (hidden * cdf).astype(BF16)
        act_ref[:, cols] = act
        slope_ref[:, cols] = (cdf + hidden * (jnp.exp(-0.5 * hidden * hidden) * INV_ROOT_TWO_PI)).astype(BF16)
        total = total + mm_nt(act, down[:, cols])
    normed, inverse = norm_rows(total)
    norm_ref[...] = normed
    inv_ref[...] = inverse
    enc = (normed * vec_ref[2:3, :] + vec_ref[3:4, :]).astype(BF16)
    enc_ref[...] = enc
    held[...] = enc.astype(F32)
    for j in range(cls_ref.shape[1]):
        cls_ref[0, j : j + 1, :] = held[pl.ds(spot_ref[step, j], 1), :]


def ffn_fwd(place, here, spots, packs, xhat, vec, bup):
    tokens, d = xhat.shape
    steps, per_row = spots.shape
    ff = bup.shape[0] * bup.shape[1]
    row = lambda width: pl.BlockSpec((FFN_ROW, width), lambda i: (i, 0))
    return pl.pallas_call(
        functools.partial(ffn_fwd_kernel, place),
        grid=(steps,),
        in_specs=[SMEM, SMEM] + [ANY] * place.count + [row(d), whole(vec.shape), whole(bup.shape)],
        out_specs=[row(ff), row(ff), row(d), row(1), row(d), pl.BlockSpec((1, per_row, d), lambda i: (i, 0, 0))],
        out_shape=[
            jax.ShapeDtypeStruct((tokens, ff), BF16),
            jax.ShapeDtypeStruct((tokens, ff), BF16),
            jax.ShapeDtypeStruct((tokens, d), F32),
            jax.ShapeDtypeStruct((tokens, 1), F32),
            jax.ShapeDtypeStruct((tokens, d), BF16),
            jax.ShapeDtypeStruct((steps, per_row, d), F32),
        ],
        scratch_shapes=[pltpu.VMEM((d, ff), BF16), pltpu.VMEM((d, ff), BF16), pltpu.VMEM((FFN_ROW, d), F32),
                        pltpu.SemaphoreType.DMA((2, place.npb))],
        compiler_params=pltpu.CompilerParams(vmem_limit_bytes=58 * MIB),
        cost_estimate=BRIEF,
        name="ffn_fwd",
    )(here, spots, *packs, xhat, vec, bup)


def loss_kernel(scale, q_count, p_count, ids_ref, own_ids_ref, heads_ref, own_ref, loss_ref, gq_ref, gp_ref):
    def split_mm(dot, left, right):
        high = left.astype(BF16)
        rest = left - high.astype(F32)
        mid = rest.astype(BF16)
        tail = (rest - mid.astype(F32)).astype(BF16)
        return dot(high, right) + dot(mid, right) + dot(tail, right)

    def put(ref, rows):
        count = ref.shape[1]
        for k in range(ref.shape[0]):
            ref[k] = rows[k * count : (k + 1) * count]

    def log_norm(scores):
        peak = jnp.max(scores, axis=1, keepdims=True)
        return peak + jnp.log(jnp.sum(jnp.exp(scores - peak), axis=1, keepdims=True))

    def parts(block):
        wide = block.astype(F32)
        d = wide.shape[-1]
        p_rows = wide[:, :p_count].reshape(-1, d).astype(BF16)
        q_rows = wide[:, p_count : p_count + q_count].reshape(-1, d).astype(BF16)
        code = wide[:, p_count + q_count :, :128].reshape(-1, 128)
        return p_rows, q_rows, (code[:, 0:1] * 256.0 + code[:, 1:2]).astype(jnp.int32)

    p_all, q_all, hit_all = parts(heads_ref[...])
    p_own, q_own, hit_own = parts(own_ref[...])
    norm_all = log_norm(mm_nt(q_all, p_all) * scale)
    own_rows = mm_nt(q_own, p_all) * scale
    norm_own = log_norm(own_rows)
    hits = ids_ref[...] == hit_own
    loss_ref[...] = norm_own - jnp.sum(jnp.where(hits, own_rows, 0.0), axis=1, keepdims=True)
    tile = jnp.exp(own_rows - norm_own) - jnp.where(hits, 1.0, 0.0)
    put(gq_ref, split_mm(mm, tile, p_all) * scale)
    own_cols = mm_nt(q_all, p_own) * scale
    hits = own_ids_ref[...] == hit_all
    tile = jnp.exp(own_cols - norm_all) - jnp.where(hits, 1.0, 0.0)
    put(gp_ref, split_mm(mm_tn, tile, q_all) * scale)


def loss_part(ids, own_ids, heads, own, q_spots, p_spots):
    d = heads.shape[2]
    q_count, p_count = math.prod(q_spots), math.prod(p_spots)
    return pl.pallas_call(
        functools.partial(loss_kernel, 3.0 / math.sqrt(d), q_count, p_count),
        out_shape=[
            jax.ShapeDtypeStruct((q_count, 1), F32),
            jax.ShapeDtypeStruct(q_spots + (d,), F32),
            jax.ShapeDtypeStruct(p_spots + (d,), F32),
        ],
        compiler_params=pltpu.CompilerParams(vmem_limit_bytes=60 * MIB),
        name="loss_part",
    )(ids, own_ids, heads, own)


def ffn_bwd_kernel(place, goal, steps, here_ref, spot_ref, *refs):
    packs, refs = refs[: place.count], refs[place.count :]
    cot_ref, gcls_ref, norm_ref, inv2_ref, act_ref, slope_ref, xhat_ref, inv1_ref, vec_ref, dh_ref = refs[:10]
    grads, refs = refs[10 : 10 + goal.count], refs[10 + goal.count :]
    gvec_ref, gbup_ref, up, down, held, first_t, down_t, hidden_all, act_all, sems = refs
    step = pl.program_id(0)
    tiles = gbup_ref.shape[0]
    ff = up.shape[1]
    width = ff // tiles

    load = FfnLoad(place, here_ref, packs, up, down, sems)

    @pl.when(step == 0)
    def _():
        load.start()
        gvec_ref[...] = jnp.zeros_like(gvec_ref)
        gbup_ref[...] = jnp.zeros_like(gbup_ref)

    @pl.when(step < steps)
    def _():
        held[...] = cot_ref[...].astype(F32)
        for j in range(gcls_ref.shape[1]):
            spot = pl.ds(spot_ref[step, j], 1)
            held[spot, :] = held[spot, :] + gcls_ref[0, j : j + 1, :]
        grad_out = held[...]
        normed = norm_ref[...]
        gvec_ref[2:3, :] += col_sum(grad_out * normed)
        gvec_ref[3:4, :] += col_sum(grad_out)
        grad_two = norm_back(grad_out, vec_ref[2:3, :], normed, inv2_ref[...])
        down_low = grad_two.astype(BF16)
        gvec_ref[7:8, :] += col_sum(down_low.astype(F32))
        tok = pl.ds(pl.multiple_of(step * FFN_ROW, FFN_ROW), FFN_ROW)
        total = grad_two
        for t in range(tiles):
            cols = slice(t * width, (t + 1) * width)

            @pl.when(step == 0)
            def _():
                load.wait(1, t)
                load.wait(0, t)

            hidden = (mm(down_low, down[:, cols]) * slope_ref[:, cols].astype(F32)).astype(BF16)
            hidden_all[tok, cols] = hidden
            gbup_ref[t : t + 1, :] += col_sum(hidden.astype(F32))
            total = total + mm_nt(hidden, up[:, cols])
        act_all[tok, :] = act_ref[...]
        xhat = xhat_ref[...]
        gvec_ref[0:1, :] += col_sum(total * xhat)
        gvec_ref[1:2, :] += col_sum(total)
        dh_ref[...] = norm_back(total, vec_ref[0:1, :], xhat, inv1_ref[...])
        first_low = (xhat * vec_ref[0:1, :] + vec_ref[1:2, :]).astype(BF16)
        for s in range(steps):
            @pl.when(step == s)
            def _():
                first_t[:, s * FFN_ROW : (s + 1) * FFN_ROW] = first_low.T
                down_t[:, s * FFN_ROW : (s + 1) * FFN_ROW] = down_low.T

    npb, npa = goal.npb, goal.npa
    r, c, dr = up.shape[0] // npb, ff // npa, up.shape[0] // npa
    part = ff // npb

    for b in range(npb):
        @pl.when(step == steps + b)
        def _():
            cols = slice(b * part, (b + 1) * part)
            up[:, cols] = mm(first_t[...], hidden_all[:, cols]).astype(BF16)

    @pl.when(step == steps + npb - 1)
    def _():
        for array, lead, base, b, a in goal.pieces(grads, 0, r, here_ref):
            pltpu.make_async_copy(up.at[span(b, r), lane_span(a, c, 0, c)], array.at[lead + (pl.ds(base, r),)],
                                  sems.at[0, 0]).start()

    for b in range(npb):
        @pl.when(step == steps + npb + b)
        def _():
            cols = slice(b * part, (b + 1) * part)
            down[:, cols] = mm(down_t[...], act_all[:, cols]).astype(BF16)

    @pl.when(step == steps + 2 * npb - 1)
    def _():
        for array, lead, base, b, a in goal.pieces(grads, 1, r, here_ref):
            for j in range(part // c):
                pltpu.make_async_copy(down.at[span(a, dr), lane_span(b, part, j * c, c)],
                                      array.at[lead + (pl.ds(base + j * dr, dr),)], sems.at[1, 0]).start()
        pltpu.make_async_copy(up, up, sems.at[0, 0]).wait()
        pltpu.make_async_copy(down, down, sems.at[1, 0]).wait()


def ffn_bwd(place, goal, here, spots, packs, cot, gcls, norm2, inv2, act, slope, xhat, inv1, vec, bup_shape):
    tokens, d = xhat.shape
    steps, per_row = spots.shape
    goal_shapes = goal.shapes(d, act.shape[1])
    ff = act.shape[1]
    last = lambda i: jnp.minimum(i, steps - 1)
    row = lambda width: pl.BlockSpec((FFN_ROW, width), lambda i: (last(i), 0))
    return pl.pallas_call(
        functools.partial(ffn_bwd_kernel, place, goal, steps),
        grid=(steps + 2 * goal.npb,),
        in_specs=[SMEM, SMEM] + [ANY] * place.count + [
            row(d), pl.BlockSpec((1, per_row, d), lambda i: (last(i), 0, 0)), row(d), row(1), row(ff), row(ff), row(d), row(1),
            whole(vec.shape)],
        out_specs=[row(d)] + [ANY] * goal.count + [whole(vec.shape), whole(bup_shape)],
        out_shape=[
            jax.ShapeDtypeStruct((tokens, d), F32),
            *goal_shapes,
            jax.ShapeDtypeStruct(vec.shape, F32),
            jax.ShapeDtypeStruct(bup_shape, F32),
        ],
        scratch_shapes=[pltpu.VMEM((d, ff), BF16), pltpu.VMEM((d, ff), BF16), pltpu.VMEM((FFN_ROW, d), F32),
                        pltpu.VMEM((d, tokens), BF16), pltpu.VMEM((d, tokens), BF16), pltpu.VMEM((tokens, ff), BF16),
                        pltpu.VMEM((tokens, ff), BF16), pltpu.SemaphoreType.DMA((2, place.npb))],
        compiler_params=pltpu.CompilerParams(vmem_limit_bytes=60 * MIB),
        cost_estimate=BRIEF,
        name="ffn_bwd",
    )(here, spots, *packs, cot, gcls, norm2, inv2, act, slope, xhat, inv1, vec)


def attn_bwd_kernel(first, dh_ref, qkv_ref, att_w_ref, segc_ref, segr_ref, gvec_in, proj_in, branch_in, proj, branch, gvec):
    d = dh_ref.shape[1]

    @pl.when(pl.program_id(0) == 0)
    def _():
        gvec[...] = gvec_in[...]

    low = dh_ref[...].astype(BF16)
    branch[...] = low
    gvec[6:7, :] += col_sum(low.astype(F32))
    att_grad = mm_nt(low, att_w_ref[...]).astype(BF16)
    blocked = jnp.where(segc_ref[0][:, 1:2] == segr_ref[0][0:1, :], 0.0, NEG_FILL)
    low_half = lax.broadcasted_iota(jnp.int32, (1, 2 * HD), 1) < HD
    keep = (low_half.astype(F32).astype(BF16), (1.0 - low_half.astype(F32)).astype(BF16))
    for p in range(d // (2 * HD)):
        lanes = slice(p * 2 * HD, (p + 1) * 2 * HD)
        k_lanes = slice(d + p * 2 * HD, d + (p + 1) * 2 * HD)
        v_lanes = slice(2 * d + p * 2 * HD, 2 * d + (p + 1) * 2 * HD)
        q2 = qkv_ref[:, lanes]
        k2 = qkv_ref[:, k_lanes]
        v2 = qkv_ref[:, v_lanes]
        g2 = att_grad[:, lanes]
        dq, dk, dv = [], [], []
        for h in range(2):
            scores = mm_nt(k2 * keep[h], q2) + blocked
            terms = jnp.exp(scores - jnp.max(scores, axis=0, keepdims=True))
            prob = terms * (1.0 / jnp.sum(terms, axis=0, keepdims=True))
            weighed = prob * mm_nt(v2 * keep[h], g2)
            sgrad = (weighed - prob * jnp.sum(weighed, axis=0, keepdims=True)).astype(BF16)
            dv.append(mm(prob.astype(BF16), g2))
            dk.append(mm(sgrad, q2))
            dq.append(mm_tn(sgrad, k2))
        proj[:, lanes] = (jnp.where(low_half, dq[0], dq[1]) * (HD ** -0.5)).astype(BF16)
        proj[:, k_lanes] = jnp.where(low_half, dk[0], dk[1]).astype(BF16)
        proj[:, v_lanes] = jnp.where(low_half, dv[0], dv[1]).astype(BF16)
    gvec[4:5, :] += col_sum(proj[:, :d].astype(F32))
    gvec[5:6, :] += col_sum(proj[:, 2 * d :].astype(F32))


def attn_bwd(first, last, dh, qkv, segc, segr, wout, gvec, before):
    tokens, d = dh.shape
    row = lambda width: pl.BlockSpec((ROW, width), lambda i: (i + first, 0))
    shapes = [jax.ShapeDtypeStruct((tokens, 3 * d), BF16), jax.ShapeDtypeStruct((tokens, d), BF16)]
    if before is None:
        kernel = lambda *refs: attn_bwd_kernel(first, *refs[:6], None, None, *refs[6:])
    else:
        kernel = lambda *refs: attn_bwd_kernel(first, *refs)
    return pl.pallas_call(
        kernel,
        grid=(last - first,),
        in_specs=[row(d), row(3 * d), whole(wout.shape), pl.BlockSpec((1, ROW, 2), lambda i: (i + first, 0, 0)),
                  pl.BlockSpec((1, 2, ROW), lambda i: (i + first, 0, 0)), whole(gvec.shape)]
        + ([] if before is None else [ANY, ANY]),
        out_specs=[row(3 * d), row(d), whole(gvec.shape)],
        out_shape=shapes + [jax.ShapeDtypeStruct(gvec.shape, F32)],
        input_output_aliases={} if before is None else {6: 0, 7: 1},
        compiler_params=pltpu.CompilerParams(vmem_limit_bytes=60 * MIB),
        cost_estimate=BRIEF,
        name="attn_bwd",
    )(dh, qkv, wout, segc, segr, gvec, *(before or ()))


def attn_grad_kernel(dims, goals, here_ref, x_ref, att_ref, proj_ref, branch_ref, gvec, gbup, *refs):
    total = goals[0][0].count
    grads, (x_t, wide, out, main, extra, sems) = refs[:total], refs[total:]
    npb, npa, r, wq, wo, rows_per, w1, w2 = dims
    step = pl.program_id(0)
    d = x_ref.shape[1]
    c = wq + wo

    def widen(piece):
        if piece.shape[1] == c:
            return piece
        return jnp.concatenate([piece, jnp.zeros((piece.shape[0], c - piece.shape[1]), F32)], axis=1)

    def multiply(g):
        wide[:, g * d : (g + 1) * d] = mm(x_t[...], proj_ref[...]).astype(BF16)

    def fill(g):
        for a in range(npa):
            if -(-(a + 1) * wq // d) == g:
                main[a] = jnp.concatenate([wide[:, a * wq : (a + 1) * wq], out[:, a * wo : (a + 1) * wo]], axis=1)

    @pl.when(step == 0)
    def _():
        x_t[...] = x_ref[...].T
        multiply(0)
        out[...] = mm(att_ref[...].T, branch_ref[...]).astype(BF16)

    for g in range(1, 3):
        @pl.when(step == g)
        def _():
            multiply(g)
            fill(g)

    @pl.when(step == 3)
    def _():
        fill(3)
        for b in range(npb):
            for a in range(npa):
                rows = [widen(gvec[b * rows_per : (b + 1) * rows_per, a * w1 : (a + 1) * w1]),
                        widen(gbup[b : b + 1, a * w2 : (a + 1) * w2]),
                        jnp.zeros((EXTRA - 1 - rows_per, c), F32)]
                extra[b * npa + a] = jnp.concatenate(rows, axis=0).astype(BF16)
        for goal, low, high in goals:
            top = min(high, r)
            for index, lead, b, a in goal.blocks(here_ref):
                target = grads[index]
                start = b * r + low
                if not isinstance(start, int):
                    start = pl.multiple_of(start, 16)
                pltpu.make_async_copy(main.at[a, pl.ds(start, top - low)], target.at[lead + (pl.ds(low, top - low),)],
                                      sems.at[0]).start()
                if high > r:
                    pltpu.make_async_copy(extra.at[b * npa + a], target.at[lead + (pl.ds(r, EXTRA),)], sems.at[1]).start()
        pltpu.make_async_copy(main, main, sems.at[0]).wait()
        pltpu.make_async_copy(extra, extra, sems.at[1]).wait()


def attn_grad(dims, goals, here, x, att, proj, branch, gvec, gbup):
    npb, npa, r, wq, wo, rows_per, w1, w2 = dims
    tokens, d = x.shape
    c = wq + wo
    return pl.pallas_call(
        functools.partial(attn_grad_kernel, dims, goals),
        grid=(4,),
        in_specs=[SMEM, whole(x.shape), whole(att.shape), pl.BlockSpec((tokens, d), lambda i: (0, jnp.minimum(i, 2))),
                  whole(branch.shape), whole(gvec.shape), whole(gbup.shape)],
        out_specs=[ANY] * goals[0][0].count,
        out_shape=[jax.ShapeDtypeStruct(goals[0][0].lead + (goals[-1][2], c), BF16)] * goals[0][0].count,
        scratch_shapes=[pltpu.VMEM((d, tokens), BF16), pltpu.VMEM((d, 3 * d), BF16), pltpu.VMEM((d, d), BF16),
                        pltpu.VMEM((npa, d, c), BF16),
                        pltpu.VMEM((npb * npa, EXTRA, c), BF16), pltpu.SemaphoreType.DMA((2,))],
        compiler_params=pltpu.CompilerParams(vmem_limit_bytes=60 * MIB),
        cost_estimate=BRIEF,
        name="attn_grad",
    )(here, x, att, proj, branch, gvec, gbup)


def input_grad_kernel(proj_ref, weight_ref, dh_ref, out_ref):
    out_ref[...] = mm_nt(proj_ref[...], weight_ref[...]) + dh_ref[...]


def input_grad(proj, wqkv, dh):
    tokens, d = dh.shape
    row = lambda width: pl.BlockSpec((ROW, width), lambda i: (i, 0))
    return pl.pallas_call(
        input_grad_kernel,
        grid=(tokens // ROW,),
        in_specs=[row(3 * d), whole(wqkv.shape), row(d)],
        out_specs=row(d),
        out_shape=jax.ShapeDtypeStruct((tokens, d), F32),
        compiler_params=pltpu.CompilerParams(vmem_limit_bytes=60 * MIB),
        cost_estimate=BRIEF,
        name="input_grad",
    )(proj, wqkv, dh)


class Blocks:
    def __init__(self, npb, npa, d, ff):
        self.npb, self.npa, self.d, self.ff = npb, npa, d, ff
        self.r, self.wq, self.wo, self.c = d // npb, 3 * d // npa, d // npa, ff // npa
        self.dr, self.dc = d // npa, ff // npb
        self.rows_per, self.w1, self.w2 = 8 // npb, d // npa, ff // (npa * npb)
        self.direct = self.c % 128 == 0 and self.r % 16 == 0 and self.dr % 16 == 0
        if self.direct:
            self.dims = (npb, npa, self.r, self.wq, self.wo, self.rows_per, self.w1, self.w2)
        else:
            self.dims = (1, 1, d, 3 * d, d, 8, d, ff)

    def pack(self, w_qkv, w_out, w_up, w_down, norm_bias, bias_up):
        c = self.wq + self.wo
        vec = jnp.pad(norm_bias, ((0, 0), (0, 0), (0, c - self.w1)))
        bup = jnp.pad(bias_up[:, None, :], ((0, 0), (0, EXTRA - 1 - self.rows_per), (0, c - self.w2)))
        attn = jnp.concatenate([jnp.concatenate([w_qkv, w_out], axis=2), vec, bup], axis=1)
        down_t = jnp.swapaxes(w_down, 1, 2)
        down = jnp.concatenate([down_t[:, :, j : j + self.c] for j in range(0, self.dc, self.c)], axis=1)
        return attn, jnp.concatenate([w_up, down], axis=1)

    def from_blocks(self, attn, ffn):
        if self.direct:
            return attn, ffn
        d, ff, r = self.d, self.ff, self.r
        rows = lambda part, height: part.transpose(0, 2, 1, 3).reshape(height, -1)
        qkv = rows(attn[:, :, :r, : self.wq], d)
        out = rows(attn[:, :, :r, self.wq :], d)
        vec = rows(attn[:, :, r : r + self.rows_per, : self.w1], 8)
        bup = attn[:, :, r + self.rows_per, : self.w2].reshape(1, ff)
        vec = jnp.pad(vec, ((0, 0), (0, 3 * d)))
        bup = jnp.pad(bup, ((0, EXTRA - 9), (0, 4 * d - ff)))
        wide = jnp.concatenate([jnp.concatenate([qkv, out], axis=1), vec, bup], axis=0)
        up = rows(ffn[:, :, :r], d)
        pieces = self.dc // self.c
        down = ffn[:, :, r:].reshape(self.npb, self.npa, pieces, self.dr, self.c)
        down = down.transpose(1, 3, 0, 2, 4).reshape(d, ff)
        return wide[None, None], jnp.concatenate([up, down])[None, None]

    def to_blocks(self, attn, ffn):
        if self.direct:
            return attn, ffn
        d, ff, npb, npa = self.d, self.ff, self.npb, self.npa
        blocks = lambda part, height: part.reshape(npb, height, npa, -1).transpose(0, 2, 1, 3)
        wide = attn[0, 0]
        c = self.wq + self.wo
        main = jnp.concatenate([blocks(wide[:d, : 3 * d], self.r), blocks(wide[:d, 3 * d :], self.r)], axis=3)
        vec = blocks(wide[d : d + 8, :d], self.rows_per)
        vec = jnp.pad(vec, ((0, 0), (0, 0), (0, 0), (0, c - self.w1)))
        bup = wide[d + 8, :ff].reshape(npb, npa, 1, self.w2)
        bup = jnp.pad(bup, ((0, 0), (0, 0), (0, EXTRA - 1 - self.rows_per), (0, c - self.w2)))
        pieces = self.dc // self.c
        down = ffn[0, 0, d:].reshape(npa, self.dr, npb, pieces, self.c).transpose(2, 0, 3, 1, 4)
        down = down.reshape(npb, npa, pieces * self.dr, self.c)
        return jnp.concatenate([main, vec, bup], axis=2), jnp.concatenate([blocks(ffn[0, 0, :d], self.r), down], axis=2)

    def unpack(self, attn, ffn):
        r = self.r
        attn, ffn = jnp.stack(attn), jnp.stack(ffn)
        down = ffn[:, r:]
        down = jnp.concatenate([down[:, j * self.dr : (j + 1) * self.dr] for j in range(self.dc // self.c)], axis=2)
        return (attn[:, :r, : self.wq], attn[:, :r, self.wq :], ffn[:, :r], jnp.swapaxes(down, 1, 2),
                attn[:, r : r + self.rows_per, : self.w1], attn[:, r + self.rows_per, : self.w2])


BOTH = ("pb", "pa")
BITS = {"core": 8, "y": 16, "z1": 2, "z2": 4, "z3": 6, "x": 1, "xy": 17}


def swap(block, way):
    return lax.ppermute(block, BOTH, [(i, i ^ BITS[way]) for i in range(32)])


class Gather:
    def __init__(self, block, ways):
        self.held, self.ways = [block], ways

    def after(self, *others):
        late = [held for other in others for held in other.held]
        self.held = list(lax.optimization_barrier((tuple(self.held), tuple(late)))[0])

    def step(self, stage):
        if stage == 0:
            block = self.held[0]
            self.held = [jnp.stack([block] + [swap(block, way) for way in ("z1", "z2", "z3")])]
        else:
            way = self.ways[stage - 1] if stage < 3 else "core"
            self.held = self.held + [swap(part, way) for part in self.held]


def gather_heads(block):
    near = jnp.stack([block] + [swap(block, way) for way in ("z1", "z2", "z3")])
    wide = jnp.stack([near] + [swap(near, way) for way in ("x", "y", "xy")])
    return jnp.stack([wide, swap(wide, "core")]).reshape((-1,) + block.shape)


HEAD_ORDER = [c ^ s ^ z for c in (0, 8) for s in (0, 1, 16, 17) for z in (0, 2, 4, 6)]


def cut_out(array, pick, rows):
    depth = len(pick)
    low = list(pick) + [0] * (array.ndim - depth)
    high = [index + 1 for index in pick] + list(array.shape[depth:])
    low[-2], high[-2] = rows.start, rows.stop
    return lax.slice(array, low, high).reshape([h - l for l, h in zip(low, high)][depth:])


class Scatter:
    def __init__(self, keep, send, cut):
        self.shared = [keep, send]
        self.own = [[], []]
        self.rows = [slice(0, cut), slice(cut, keep.shape[-2])]
        self.spot = ()

    def sum(self, part, j=None):
        pick = self.spot if j is None else self.spot + (j,)
        terms = [cut_out(array, pick, self.rows[part]) for array in self.shared]
        for age, array in self.own[part]:
            terms.append(cut_out(array, pick[age:], slice(0, array.shape[-2])))
        return sum(term.astype(F32) for term in terms)

    def step(self, stage, line):
        if stage == 0:
            self.shared = [self.shared[0], swap(line.wait((self.shared[1],))[0], "core")]
            return
        self.fresh(line)
        if stage < 3:
            parts = [self.sum(part, 1).astype(BF16) for part in range(2)]
            line.mark(parts)
            self.spot += (0,)
            for part, ways in enumerate((("y", "x"), ("x", "y"))):
                self.own[part].append((len(self.spot), swap(parts[part], ways[stage - 1])))
            return
        parts = [jnp.concatenate([self.sum(part, j) for part in range(2)]).astype(BF16) for j in range(1, 4)]
        line.mark(parts)
        self.spot += (0,)
        self.last = [swap(part, f"z{j + 1}") for j, part in enumerate(parts)]

    def fresh(self, line):
        if self.spot:
            arrays = line.wait(tuple(own[-1][1] for own in self.own))
            for own, array in zip(self.own, arrays):
                own[-1] = (own[-1][0], array)
        else:
            self.shared[1] = line.wait((self.shared[1],))[0]

    def total(self, line):
        last = line.wait(tuple(self.last))
        kept = jnp.concatenate([self.sum(part) for part in range(2)])
        return line.mark(kept + sum(term.astype(F32) for term in last))


class Line:
    def __init__(self):
        self.last = None

    def wait(self, operands):
        if self.last is None:
            return operands
        return lax.optimization_barrier((operands, self.last))[0]

    def mark(self, result):
        self.last = jax.tree.leaves(result)[0]
        return result

    def run(self, step, *operands):
        return self.mark(step(*self.wait(operands)))


def body(questions, passages, cot_questions, cot_passages, question_lengths, segment_lengths, positives, w_qkv, w_out, w_up,
         w_down, norm_bias, bias_up):
    q_count, q_len, d = questions.shape
    row_count, row_len, _ = passages.shape
    segs = segment_lengths.shape[1]
    npb, npa = lax.axis_size("pb"), lax.axis_size("pa")
    size = Blocks(npb, npa, d, bias_up.shape[1] * npb * npa)
    dims = size.dims
    near = size.direct and (npb, npa) == (4, 8)
    pb, pa = lax.axis_index("pb"), lax.axis_index("pa")
    device = pb * npa + pa
    here = jnp.stack([pb // 2, pb % 2, pa // 2, pa % 2]).astype(jnp.int32)
    order = (("y", "x"), ("x", "y"))

    attn_pack, ffn_pack = size.pack(w_qkv, w_out, w_up, w_down, norm_bias, bias_up)
    mesh_order = Place(dims[0], dims[1], None, False)
    one_array = FfnPlace(mesh_order)
    if near:
        ffn_all = lax.all_gather(ffn_pack, BOTH, axis=0).reshape((npb, npa) + ffn_pack.shape)
        parts = [Gather(attn_pack[e], order[e]) for e in range(2)]
        for stage in range(4):
            for each in parts:
                each.step(stage)
        attn_w = [each.held for each in parts]
        attn_into = [Place(npb, npa, order[e][0], True) for e in range(2)]
        ffn_w = [[ffn_all]] * 2
        ffn_into = [FfnPlace(mesh_order, e=e) for e in range(2)]
    else:
        attn_all = lax.all_gather(attn_pack, BOTH, axis=0).reshape((npb, npa) + attn_pack.shape)
        ffn_all = lax.all_gather(ffn_pack, BOTH, axis=0).reshape((npb, npa) + ffn_pack.shape)
        attn_w, ffn_w = zip(*[size.from_blocks(attn_all[:, :, e], ffn_all[:, :, e]) for e in range(2)])
        attn_w = [[blocks] for blocks in attn_w]
        ffn_w = [[blocks] for blocks in ffn_w]
        attn_into = [mesh_order] * 2
        ffn_into = [one_array] * 2

    per_row = ROW // q_len
    q_rows = q_count // per_row
    token = jnp.arange(ROW, dtype=jnp.int32)
    q_seg = jnp.broadcast_to(token // q_len, (q_rows, ROW))
    q_valid = (token % q_len)[None, :] < jnp.repeat(question_lengths.reshape(q_rows, per_row), q_len, axis=1)
    starts = jnp.cumsum(segment_lengths, axis=1) - segment_lengths
    p_seg = jnp.sum((token[None, None, :] >= starts[:, :, None]).astype(jnp.int32), axis=1)
    segr = (jnp.stack([q_seg, jnp.where(q_valid, q_seg, -1)], axis=1), jnp.stack([p_seg, p_seg], axis=1))
    segc = tuple(jnp.swapaxes(pair, 1, 2) for pair in segr)
    spots = (jnp.broadcast_to(jnp.arange(per_row, dtype=jnp.int32) * q_len, (q_rows, per_row)), starts)
    xs = (questions.reshape(-1, d), passages.reshape(-1, d))
    cots = [cot_questions.reshape(-1, d), cot_passages.reshape(-1, d)]
    p_count = row_count * segs

    def by_step(spots):
        rows = FFN_ROW // ROW
        base = jnp.arange(spots.shape[0], dtype=jnp.int32) % rows * ROW
        return (spots + base[:, None]).reshape(-1, rows * spots.shape[1])

    spots = tuple(by_step(each) for each in spots)
    own_hits = lax.dynamic_slice_in_dim(positives, pa * q_count, q_count)
    code = jnp.pad(jnp.stack([own_hits // 256, own_hits % 256], axis=1).astype(BF16), ((0, 0), (0, d - 2)))
    listed = device ^ jnp.array(HEAD_ORDER, jnp.int32) if near else jnp.arange(npb * npa, dtype=jnp.int32)
    ids = (listed[:, None] * p_count + jnp.arange(p_count, dtype=jnp.int32)[None, :]).reshape(1, -1)
    own_ids = device * p_count + jnp.arange(p_count, dtype=jnp.int32)[None, :]

    line = Line()
    half = [
        line.run(lambda x, *packs, e=e: attn_fwd(dims, attn_into[e], here, packs, x, segc[e], segr[e]), xs[e], *attn_w[e])
        for e in range(2)
    ]
    done = [None, None]
    for e in (0, 1):
        done[e] = line.run(
            lambda *packs, e=e: ffn_fwd(ffn_into[e], here, spots[e], packs, half[e][2], half[e][6], half[e][7]), *ffn_w[e])
    own = jnp.concatenate([done[1][5].reshape(p_count, d).astype(BF16), done[0][5].reshape(q_count, d).astype(BF16), code])
    heads = gather_heads(own) if near else lax.all_gather(own, BOTH, axis=0)
    losses, *gcls = loss_part(ids, own_ids, heads, own[None], spots[0].shape, spots[1].shape)

    def ffn_step(e, goal, cot):
        _, _, xhat, inv1, _, _, vec, bup = half[e]
        act, slope, norm2, inv2, _, _ = done[e]
        dh, *blocks, gvec, gbup = ffn_bwd(ffn_into[e], goal, here, spots[e], ffn_w[e], cot, gcls[e], norm2,
                                          inv2, act, slope, xhat, inv1, vec, bup.shape)
        return dh, blocks, gvec, gbup

    def attn_rows(e, first, last, dh, gvec, before):
        return attn_bwd(first, last, dh, half[e][0], segc[e], segr[e], half[e][5], gvec, before)

    def attn_weights(e, goals, rows, gbup):
        return attn_grad(dims, goals, here, xs[e], half[e][1], rows[0], rows[1], rows[2], gbup)

    def scatter(blocks, dtype=F32):
        flat = blocks.reshape((npb * npa,) + blocks.shape[2:])
        return lax.psum_scatter(flat, BOTH, scatter_dimension=0, tiled=False).astype(dtype)

    counts = (q_rows, row_count)
    if near:
        whole_block = attn_pack.shape[1]
        cut = whole_block // 32 * 16 + 16
        y_first, x_first = (Place(npb, npa, way[0], False) for way in order)
        goals = [(y_first, 0, cut), (x_first, cut, whole_block)]
        line = Line()
        dh_q, blocks_q, gvec_q, gbup_q = line.run(lambda cot: ffn_step(0, one_array, cot), cots[0])
        sum_q = scatter(blocks_q[0], BF16)
        dh_p, blocks_p, gvec_p, gbup_p = line.run(lambda cot: ffn_step(1, FfnPlace(y_first, x_first), cot), cots[1])
        ffn_p = Scatter(*blocks_p, size.r)
        ffn_p.step(0, line)
        rows_q = line.run(lambda dh: attn_rows(0, 0, q_rows, dh, gvec_q, None), dh_q)
        ffn_p.step(1, line)
        attn_q = Scatter(*line.run(lambda *rows: attn_weights(0, goals, rows, gbup_q), *rows_q), cut)
        middle = row_count // 2
        rows_p = line.run(lambda dh: attn_rows(1, 0, middle, dh, gvec_p, None), dh_p)
        ffn_p.step(2, line)
        attn_q.step(0, line)
        rows_p = line.run(lambda *rows: attn_rows(1, middle, row_count, dh_p, rows[2], rows[:2]), *rows_p)
        ffn_p.step(3, line)
        attn_q.step(1, line)
        attn_p = Scatter(*line.run(lambda *rows: attn_weights(1, goals, rows, gbup_p), *rows_p), cut)
        attn_q.step(2, line)
        attn_p.step(0, line)
        gx_q = line.run(lambda proj: input_grad(proj, half[0][4], dh_q), rows_q[0])
        attn_p.step(1, line)
        attn_q.step(3, line)
        gx_p = line.run(lambda proj: input_grad(proj, half[1][4], dh_p), rows_p[0])
        gx = (gx_q, gx_p)
        attn_p.step(2, line)
        attn_p.step(3, line)
        sums = [ffn_p.total(line), attn_q.total(line)]
        sum_q = line.wait((sum_q,))[0]
        sums.append(attn_p.total(line))
        ffn_sum = [sum_q.astype(F32), sums[0]]
        attn_sum = sums[1:]
    else:
        pairs, gx = [], []
        for e in range(2):
            dh, blocks, gvec, gbup = ffn_step(e, one_array, cots[e])
            rows = attn_rows(e, 0, counts[e], dh, gvec, None)
            got = attn_weights(e, [(mesh_order, 0, dims[2] + EXTRA)], rows, gbup)
            pairs.append(size.to_blocks(got[0], blocks[0]))
            gx.append(input_grad(rows[0], half[e][4], dh))
        attn_sum = [scatter(pair[0]) for pair in pairs]
        ffn_sum = [scatter(pair[1]) for pair in pairs]
    outs = size.unpack(attn_sum, ffn_sum)
    return (
        done[0][4].reshape(questions.shape),
        done[1][4].reshape(passages.shape),
        losses[:, 0],
        gx[0].reshape(questions.shape),
        gx[1].reshape(passages.shape),
    ) + outs


def solution(mesh):
    rows = P(BOTH, None, None)
    shard = P(None, "pb", "pa")
    vector = P(None, BOTH)
    in_specs = (rows, rows, rows, rows, P(BOTH), P(BOTH, None), P("pb"), shard, shard, shard, shard, shard, vector)
    out_specs = (rows, rows, P(BOTH), rows, rows, shard, shard, shard, shard, shard, vector)
    return jax.shard_map(body, mesh=mesh, in_specs=in_specs, out_specs=out_specs, check_vma=False)
```

```python
import functools
import math

import jax
import jax.numpy as jnp
from jax import lax
from jax.experimental import pallas as pl
from jax.experimental.pallas import tpu as pltpu
from jax.sharding import PartitionSpec as P

HD = 64
EXTRA = 16
ROW = 256
FFN_ROW = 256
NEG_FILL = -1000000000.0
EPSILON = 1e-06
ROOT_HALF = 0.7071067811865476
INV_ROOT_TWO_PI = 0.3989422804014327
F32 = jnp.float32
BF16 = jnp.bfloat16
MIB = 1 << 20
ANY = pl.BlockSpec(memory_space=pl.ANY)
SMEM = pl.BlockSpec(memory_space=pltpu.SMEM)
BRIEF = pl.CostEstimate(flops=1, transcendentals=0, bytes_accessed=1)


def mm(left, right):
    return lax.dot_general(left, right, (((1,), (0,)), ((), ())), preferred_element_type=F32)


def mm_nt(left, right):
    return lax.dot_general(left, right, (((1,), (1,)), ((), ())), preferred_element_type=F32)


def mm_tn(left, right):
    return lax.dot_general(left, right, (((0,), (0,)), ((), ())), preferred_element_type=F32)


def whole(shape):
    return pl.BlockSpec(shape, lambda i: (0,) * len(shape), pipeline_mode=pl.Buffered(1))


def norm_rows(summed):
    centred = summed - jnp.mean(summed, axis=-1, keepdims=True)
    inverse = lax.rsqrt(jnp.mean(centred * centred, axis=-1, keepdims=True) + EPSILON)
    return centred * inverse, inverse


def norm_back(grad_out, gain, normed, inverse):
    scaled = grad_out * gain
    inner = (
        scaled
        - jnp.mean(scaled, axis=-1, keepdims=True)
        - normed * jnp.mean(scaled * normed, axis=-1, keepdims=True)
    )
    return inverse * inner


def col_sum(block):
    return jnp.sum(block, axis=0, keepdims=True)


class Place:
    def __init__(self, npb, npa, first, into):
        self.npb, self.npa, self.first, self.into = npb, npa, first, into
        self.count = 1 if first is None else 8 if into else 2
        self.lead = (npb, npa) if first is None else (4,) if into else (2, 2, 4)

    def blocks(self, spot):
        if self.first is None:
            return [(0, (b, a), b, a) for b in range(self.npb) for a in range(self.npa)]
        y, core, z, x = (spot[k] for k in range(4))
        found = []
        for core_d in range(2):
            for second in range(2):
                for first in range(2):
                    for z_d in range(4):
                        y_d, x_d = (first, second) if self.first == "y" else (second, first)
                        index = core_d * 4 + second * 2 + first if self.into else core_d
                        lead = (z_d,) if self.into else (first, second, z_d)
                        b = lax.bitwise_xor(y, y_d) * 2 + lax.bitwise_xor(core, core_d)
                        a = lax.bitwise_xor(z, z_d) * 2 + lax.bitwise_xor(x, x_d)
                        found.append((index, lead, b, a))
        return found


def span(index, length):
    start = index * length
    if isinstance(start, int):
        return pl.ds(start, length)
    return pl.ds(pl.multiple_of(start, math.gcd(length, 1 << 20)), length)


def lane_span(index, stride, base, length):
    start = index * stride + base
    if isinstance(start, int):
        return pl.ds(start, length)
    return pl.ds(pl.multiple_of(start, 128), length)


def attn_fwd_kernel(dims, place, here_ref, *refs):
    packs, refs = refs[: place.count], refs[place.count :]
    (x_ref, segc_ref, segr_ref, qkv_ref, att_ref, xhat_ref, inv_ref, wqkv_ref, wout_ref, vec_ref, bup_ref, held, sem) = refs
    npb, npa, r, wq, wo, rows_per, w1, w2 = dims
    d = x_ref.shape[1]

    @pl.when(pl.program_id(0) == 0)
    def _():
        for index, lead, b, a in place.blocks(here_ref):
            pltpu.make_async_copy(packs[index].at[lead], held.at[b, a], sem).start()
        pltpu.make_async_copy(held, held, sem).wait()
        for b in range(npb):
            rows = pl.ds(b * r, r)
            wqkv_ref[rows, :] = jnp.concatenate([held[b, a, :r, :wq] for a in range(npa)], axis=1)
            wout_ref[rows, :] = jnp.concatenate([held[b, a, :r, wq:] for a in range(npa)], axis=1)
            extra = [held[b, a, r:, :].astype(F32) for a in range(npa)]
            vec_ref[pl.ds(b * rows_per, rows_per), :] = jnp.concatenate(
                [part[:rows_per, :w1] for part in extra], axis=1)
            bup_ref[b : b + 1, :] = jnp.concatenate(
                [part[rows_per : rows_per + 1, :w2] for part in extra], axis=1)

    flat = x_ref[...]
    qkv_ref[:, :d] = ((mm(flat, wqkv_ref[:, :d]) + vec_ref[4:5, :]).astype(BF16) * BF16(HD ** -0.5))
    qkv_ref[:, d : 2 * d] = mm(flat, wqkv_ref[:, d : 2 * d]).astype(BF16)
    qkv_ref[:, 2 * d :] = (mm(flat, wqkv_ref[:, 2 * d :]) + vec_ref[5:6, :]).astype(BF16)
    blocked = jnp.where(segc_ref[0][:, 0:1] == segr_ref[0][1:2, :], 0.0, NEG_FILL)
    low_half = lax.broadcasted_iota(jnp.int32, (1, 2 * HD), 1) < HD
    keep = (low_half.astype(F32).astype(BF16), (1.0 - low_half.astype(F32)).astype(BF16))
    for p in range(d // (2 * HD)):
        lanes = slice(p * 2 * HD, (p + 1) * 2 * HD)
        q2 = qkv_ref[:, lanes]
        k2 = qkv_ref[:, d + p * 2 * HD : d + (p + 1) * 2 * HD]
        v2 = qkv_ref[:, 2 * d + p * 2 * HD : 2 * d + (p + 1) * 2 * HD]
        parts = []
        for h in range(2):
            scores = mm_nt(q2 * keep[h], k2) + blocked
            terms = jnp.exp(scores - jnp.max(scores, axis=-1, keepdims=True))
            total = jnp.sum(terms, axis=-1, keepdims=True)
            prob = (terms * (1.0 / total)).astype(BF16)
            parts.append(mm(prob, v2))
        att_ref[:, lanes] = jnp.where(low_half, parts[0], parts[1]).astype(BF16)
    branch = mm(att_ref[...], wout_ref[...]) + vec_ref[6:7, :]
    normed, inverse = norm_rows(flat.astype(F32) + branch)
    xhat_ref[...] = normed
    inv_ref[...] = inverse


def attn_fwd(dims, place, here, packs, x, segc, segr):
    npb, npa, r, wq, wo, rows_per, w1, w2 = dims
    tokens, d = x.shape
    steps = tokens // ROW
    ff = w2 * npa * npb
    row = lambda width: pl.BlockSpec((ROW, width), lambda i: (i, 0))
    return pl.pallas_call(
        functools.partial(attn_fwd_kernel, dims, place),
        grid=(steps,),
        in_specs=[SMEM] + [ANY] * place.count + [row(d), pl.BlockSpec((1, ROW, 2), lambda i: (i, 0, 0)),
                  pl.BlockSpec((1, 2, ROW), lambda i: (i, 0, 0))],
        out_specs=[row(3 * d), row(d), row(d), row(1), whole((d, 3 * d)), whole((d, d)), whole((8, d)),
                   whole((npb, ff // npb))],
        out_shape=[
            jax.ShapeDtypeStruct((tokens, 3 * d), BF16),
            jax.ShapeDtypeStruct((tokens, d), BF16),
            jax.ShapeDtypeStruct((tokens, d), F32),
            jax.ShapeDtypeStruct((tokens, 1), F32),
            jax.ShapeDtypeStruct((d, 3 * d), BF16),
            jax.ShapeDtypeStruct((d, d), BF16),
            jax.ShapeDtypeStruct((8, d), F32),
            jax.ShapeDtypeStruct((npb, ff // npb), F32),
        ],
        scratch_shapes=[pltpu.VMEM((npb, npa, r + EXTRA, wq + wo), BF16), pltpu.SemaphoreType.DMA],
        compiler_params=pltpu.CompilerParams(vmem_limit_bytes=58 * MIB),
        cost_estimate=BRIEF,
        name="attn_fwd",
    )(here, *packs, x, segc, segr)


class FfnPlace:
    def __init__(self, up, down=None, e=None):
        self.up, self.down, self.e = up, down or up, e
        self.npb, self.npa, self.count = up.npb, up.npa, up.count

    def shapes(self, d, ff):
        block = (d // self.npb * 2, ff // self.npa)
        return [jax.ShapeDtypeStruct(self.up.lead + block, BF16)] * self.count

    def pieces(self, arrays, which, rows, spot):
        place = self.down if which else self.up
        extra = () if self.e is None else (self.e,)
        return [(arrays[index], lead + extra, rows if which else 0, b, a) for index, lead, b, a in place.blocks(spot)]


class FfnLoad:
    def __init__(self, place, spot, packs, up, down, sems):
        self.place, self.spot, self.packs, self.up, self.down, self.sems = place, spot, packs, up, down, sems

    def start(self):
        npb, npa = self.place.npb, self.place.npa
        d, ff = self.up.shape
        r, c, dr, dc = d // npb, ff // npa, d // npa, ff // npb
        ups = self.place.pieces(self.packs, 0, r, self.spot)
        downs = self.place.pieces(self.packs, 1, r, self.spot)
        if self.place.up.first is None:
            downs = sorted(downs, key=lambda piece: piece[3])
            ups = sorted(ups, key=lambda piece: piece[4])
        for k in range(len(ups)):
            array, lead, base, b, a = ups[k]
            pltpu.make_async_copy(array.at[lead + (pl.ds(base, r),)], self.up.at[span(b, r), lane_span(a, c, 0, c)],
                                  self.sems.at[0, a * npb // npa]).start()
            array, lead, base, b, a = downs[k]
            for j in range(dc // c):
                pltpu.make_async_copy(array.at[lead + (pl.ds(base + j * dr, dr),)],
                                      self.down.at[span(a, dr), lane_span(b, dc, j * c, c)], self.sems.at[1, b]).start()

    def wait(self, which, t):
        ref = self.down if which else self.up
        width = ref.shape[1] // self.place.npb
        part = ref.at[:, pl.ds(t * width, width)]
        pltpu.make_async_copy(part, part, self.sems.at[which, t]).wait()


def ffn_fwd_kernel(place, here_ref, spot_ref, *refs):
    packs, refs = refs[: place.count], refs[place.count :]
    (xhat_ref, vec_ref, bup_ref, act_ref, slope_ref, norm_ref, inv_ref, enc_ref, cls_ref, up, down, held, sems) = refs
    step = pl.program_id(0)

    load = FfnLoad(place, here_ref, packs, up, down, sems)

    @pl.when(step == 0)
    def _():
        load.start()

    ff = up.shape[1]
    tiles = bup_ref.shape[0]
    width = ff // tiles
    first_norm = xhat_ref[...] * vec_ref[0:1, :] + vec_ref[1:2, :]
    first_low = first_norm.astype(BF16)
    total = first_norm + vec_ref[7:8, :]
    for t in range(tiles):
        cols = slice(t * width, (t + 1) * width)

        @pl.when(step == 0)
        def _():
            load.wait(0, t)
            load.wait(1, t)

        hidden = mm(first_low, up[:, cols]) + bup_ref[t : t + 1, :]
        cdf = 0.5 + 0.5 * lax.erf(hidden * ROOT_HALF)
        act = (hidden * cdf).astype(BF16)
        act_ref[:, cols] = act
        slope_ref[:, cols] = (cdf + hidden * (jnp.exp(-0.5 * hidden * hidden) * INV_ROOT_TWO_PI)).astype(BF16)
        total = total + mm_nt(act, down[:, cols])
    normed, inverse = norm_rows(total)
    norm_ref[...] = normed
    inv_ref[...] = inverse
    enc = (normed * vec_ref[2:3, :] + vec_ref[3:4, :]).astype(BF16)
    enc_ref[...] = enc
    held[...] = enc.astype(F32)
    for j in range(cls_ref.shape[1]):
        cls_ref[0, j : j + 1, :] = held[pl.ds(spot_ref[step, j], 1), :]


def ffn_fwd(place, here, spots, packs, xhat, vec, bup):
    tokens, d = xhat.shape
    steps, per_row = spots.shape
    ff = bup.shape[0] * bup.shape[1]
    row = lambda width: pl.BlockSpec((FFN_ROW, width), lambda i: (i, 0))
    return pl.pallas_call(
        functools.partial(ffn_fwd_kernel, place),
        grid=(steps,),
        in_specs=[SMEM, SMEM] + [ANY] * place.count + [row(d), whole(vec.shape), whole(bup.shape)],
        out_specs=[row(ff), row(ff), row(d), row(1), row(d), pl.BlockSpec((1, per_row, d), lambda i: (i, 0, 0))],
        out_shape=[
            jax.ShapeDtypeStruct((tokens, ff), BF16),
            jax.ShapeDtypeStruct((tokens, ff), BF16),
            jax.ShapeDtypeStruct((tokens, d), F32),
            jax.ShapeDtypeStruct((tokens, 1), F32),
            jax.ShapeDtypeStruct((tokens, d), BF16),
            jax.ShapeDtypeStruct((steps, per_row, d), F32),
        ],
        scratch_shapes=[pltpu.VMEM((d, ff), BF16), pltpu.VMEM((d, ff), BF16), pltpu.VMEM((FFN_ROW, d), F32),
                        pltpu.SemaphoreType.DMA((2, place.npb))],
        compiler_params=pltpu.CompilerParams(vmem_limit_bytes=58 * MIB),
        cost_estimate=BRIEF,
        name="ffn_fwd",
    )(here, spots, *packs, xhat, vec, bup)


def loss_kernel(scale, q_count, p_count, ids_ref, own_ids_ref, own_ref, *refs):
    *heads, loss_ref, gq_ref, gp_ref = refs

    def split_mm(dot, left, right):
        high = left.astype(BF16)
        rest = left - high.astype(F32)
        mid = rest.astype(BF16)
        tail = (rest - mid.astype(F32)).astype(BF16)
        return dot(high, right) + dot(mid, right) + dot(tail, right)

    def put(ref, rows):
        count = ref.shape[1]
        for k in range(ref.shape[0]):
            ref[k] = rows[k * count : (k + 1) * count]

    def log_norm(scores):
        peak = jnp.max(scores, axis=1, keepdims=True)
        return peak + jnp.log(jnp.sum(jnp.exp(scores - peak), axis=1, keepdims=True))

    def parts(block):
        wide = block.astype(F32)
        d = wide.shape[-1]
        p_rows = wide[:, :p_count].reshape(-1, d).astype(BF16)
        q_rows = wide[:, p_count : p_count + q_count].reshape(-1, d).astype(BF16)
        code = wide[:, p_count + q_count :, :128].reshape(-1, 128)
        return p_rows, q_rows, (code[:, 0:1] * 256.0 + code[:, 1:2]).astype(jnp.int32)

    p_all, q_all, hit_all = parts(jnp.concatenate([ref[...] for ref in heads]))
    p_own, q_own, hit_own = parts(own_ref[...])
    norm_all = log_norm(mm_nt(q_all, p_all) * scale)
    own_rows = mm_nt(q_own, p_all) * scale
    norm_own = log_norm(own_rows)
    hits = ids_ref[...] == hit_own
    loss_ref[...] = norm_own - jnp.sum(jnp.where(hits, own_rows, 0.0), axis=1, keepdims=True)
    tile = jnp.exp(own_rows - norm_own) - jnp.where(hits, 1.0, 0.0)
    put(gq_ref, split_mm(mm, tile, p_all) * scale)
    own_cols = mm_nt(q_all, p_own) * scale
    hits = own_ids_ref[...] == hit_all
    tile = jnp.exp(own_cols - norm_all) - jnp.where(hits, 1.0, 0.0)
    put(gp_ref, split_mm(mm_tn, tile, q_all) * scale)


def loss_part(ids, own_ids, heads, own, q_spots, p_spots):
    d = own.shape[2]
    q_count, p_count = math.prod(q_spots), math.prod(p_spots)
    return pl.pallas_call(
        functools.partial(loss_kernel, 3.0 / math.sqrt(d), q_count, p_count),
        out_shape=[
            jax.ShapeDtypeStruct((q_count, 1), F32),
            jax.ShapeDtypeStruct(q_spots + (d,), F32),
            jax.ShapeDtypeStruct(p_spots + (d,), F32),
        ],
        compiler_params=pltpu.CompilerParams(vmem_limit_bytes=60 * MIB),
        name="loss_part",
    )(ids, own_ids, own, *heads)


def ffn_bwd_kernel(place, goal, steps, here_ref, spot_ref, *refs):
    packs, refs = refs[: place.count], refs[place.count :]
    cot_ref, gcls_ref, norm_ref, inv2_ref, act_ref, slope_ref, xhat_ref, inv1_ref, vec_ref, dh_ref = refs[:10]
    grads, refs = refs[10 : 10 + goal.count], refs[10 + goal.count :]
    gvec_ref, gbup_ref, up, down, held, first_t, down_t, hidden_all, act_all, sems = refs
    step = pl.program_id(0)
    tiles = gbup_ref.shape[0]
    ff = up.shape[1]
    width = ff // tiles

    load = FfnLoad(place, here_ref, packs, up, down, sems)

    @pl.when(step == 0)
    def _():
        load.start()
        gvec_ref[...] = jnp.zeros_like(gvec_ref)
        gbup_ref[...] = jnp.zeros_like(gbup_ref)

    @pl.when(step < steps)
    def _():
        held[...] = cot_ref[...].astype(F32)
        for j in range(gcls_ref.shape[1]):
            spot = pl.ds(spot_ref[step, j], 1)
            held[spot, :] = held[spot, :] + gcls_ref[0, j : j + 1, :]
        grad_out = held[...]
        normed = norm_ref[...]
        gvec_ref[2:3, :] += col_sum(grad_out * normed)
        gvec_ref[3:4, :] += col_sum(grad_out)
        grad_two = norm_back(grad_out, vec_ref[2:3, :], normed, inv2_ref[...])
        down_low = grad_two.astype(BF16)
        gvec_ref[7:8, :] += col_sum(down_low.astype(F32))
        tok = pl.ds(pl.multiple_of(step * FFN_ROW, FFN_ROW), FFN_ROW)
        total = grad_two
        for t in range(tiles):
            cols = slice(t * width, (t + 1) * width)

            @pl.when(step == 0)
            def _():
                load.wait(1, t)
                load.wait(0, t)

            hidden = (mm(down_low, down[:, cols]) * slope_ref[:, cols].astype(F32)).astype(BF16)
            hidden_all[tok, cols] = hidden
            gbup_ref[t : t + 1, :] += col_sum(hidden.astype(F32))
            total = total + mm_nt(hidden, up[:, cols])
        act_all[tok, :] = act_ref[...]
        xhat = xhat_ref[...]
        gvec_ref[0:1, :] += col_sum(total * xhat)
        gvec_ref[1:2, :] += col_sum(total)
        dh_ref[...] = norm_back(total, vec_ref[0:1, :], xhat, inv1_ref[...])
        first_low = (xhat * vec_ref[0:1, :] + vec_ref[1:2, :]).astype(BF16)
        for s in range(steps):
            @pl.when(step == s)
            def _():
                first_t[:, s * FFN_ROW : (s + 1) * FFN_ROW] = first_low.T
                down_t[:, s * FFN_ROW : (s + 1) * FFN_ROW] = down_low.T

    npb, npa = goal.npb, goal.npa
    r, c, dr = up.shape[0] // npb, ff // npa, up.shape[0] // npa
    part = ff // npb

    for b in range(npb):
        @pl.when(step == steps + b)
        def _():
            cols = slice(b * part, (b + 1) * part)
            up[:, cols] = mm(first_t[...], hidden_all[:, cols]).astype(BF16)

    @pl.when(step == steps + npb - 1)
    def _():
        for array, lead, base, b, a in goal.pieces(grads, 0, r, here_ref):
            pltpu.make_async_copy(up.at[span(b, r), lane_span(a, c, 0, c)], array.at[lead + (pl.ds(base, r),)],
                                  sems.at[0, 0]).start()

    for b in range(npb):
        @pl.when(step == steps + npb + b)
        def _():
            cols = slice(b * part, (b + 1) * part)
            down[:, cols] = mm(down_t[...], act_all[:, cols]).astype(BF16)

    @pl.when(step == steps + 2 * npb - 1)
    def _():
        for array, lead, base, b, a in goal.pieces(grads, 1, r, here_ref):
            for j in range(part // c):
                pltpu.make_async_copy(down.at[span(a, dr), lane_span(b, part, j * c, c)],
                                      array.at[lead + (pl.ds(base + j * dr, dr),)], sems.at[1, 0]).start()
        pltpu.make_async_copy(up, up, sems.at[0, 0]).wait()
        pltpu.make_async_copy(down, down, sems.at[1, 0]).wait()


def ffn_bwd(place, goal, here, spots, packs, cot, gcls, norm2, inv2, act, slope, xhat, inv1, vec, bup_shape):
    tokens, d = xhat.shape
    steps, per_row = spots.shape
    goal_shapes = goal.shapes(d, act.shape[1])
    ff = act.shape[1]
    last = lambda i: jnp.minimum(i, steps - 1)
    row = lambda width: pl.BlockSpec((FFN_ROW, width), lambda i: (last(i), 0))
    return pl.pallas_call(
        functools.partial(ffn_bwd_kernel, place, goal, steps),
        grid=(steps + 2 * goal.npb,),
        in_specs=[SMEM, SMEM] + [ANY] * place.count + [
            row(d), pl.BlockSpec((1, per_row, d), lambda i: (last(i), 0, 0)), row(d), row(1), row(ff), row(ff), row(d), row(1),
            whole(vec.shape)],
        out_specs=[row(d)] + [ANY] * goal.count + [whole(vec.shape), whole(bup_shape)],
        out_shape=[
            jax.ShapeDtypeStruct((tokens, d), F32),
            *goal_shapes,
            jax.ShapeDtypeStruct(vec.shape, F32),
            jax.ShapeDtypeStruct(bup_shape, F32),
        ],
        scratch_shapes=[pltpu.VMEM((d, ff), BF16), pltpu.VMEM((d, ff), BF16), pltpu.VMEM((FFN_ROW, d), F32),
                        pltpu.VMEM((d, tokens), BF16), pltpu.VMEM((d, tokens), BF16), pltpu.VMEM((tokens, ff), BF16),
                        pltpu.VMEM((tokens, ff), BF16), pltpu.SemaphoreType.DMA((2, place.npb))],
        compiler_params=pltpu.CompilerParams(vmem_limit_bytes=60 * MIB),
        cost_estimate=BRIEF,
        name="ffn_bwd",
    )(here, spots, *packs, cot, gcls, norm2, inv2, act, slope, xhat, inv1, vec)


def attn_bwd_kernel(first, dh_ref, qkv_ref, att_w_ref, segc_ref, segr_ref, gvec_in, proj_in, branch_in, proj, branch, gvec):
    d = dh_ref.shape[1]

    @pl.when(pl.program_id(0) == 0)
    def _():
        gvec[...] = gvec_in[...]

    low = dh_ref[...].astype(BF16)
    branch[...] = low
    gvec[6:7, :] += col_sum(low.astype(F32))
    att_grad = mm_nt(low, att_w_ref[...]).astype(BF16)
    blocked = jnp.where(segc_ref[0][:, 1:2] == segr_ref[0][0:1, :], 0.0, NEG_FILL)
    low_half = lax.broadcasted_iota(jnp.int32, (1, 2 * HD), 1) < HD
    keep = (low_half.astype(F32).astype(BF16), (1.0 - low_half.astype(F32)).astype(BF16))
    for p in range(d // (2 * HD)):
        lanes = slice(p * 2 * HD, (p + 1) * 2 * HD)
        k_lanes = slice(d + p * 2 * HD, d + (p + 1) * 2 * HD)
        v_lanes = slice(2 * d + p * 2 * HD, 2 * d + (p + 1) * 2 * HD)
        q2 = qkv_ref[:, lanes]
        k2 = qkv_ref[:, k_lanes]
        v2 = qkv_ref[:, v_lanes]
        g2 = att_grad[:, lanes]
        dq, dk, dv = [], [], []
        q_t, k_t, g_t = q2.T, k2.T, g2.T
        for h in range(2):
            scores = mm(k2 * keep[h], q_t) + blocked
            terms = jnp.exp(scores - jnp.max(scores, axis=0, keepdims=True))
            prob = terms * (1.0 / jnp.sum(terms, axis=0, keepdims=True))
            weighed = prob * mm(v2 * keep[h], g_t)
            sgrad = (weighed - prob * jnp.sum(weighed, axis=0, keepdims=True)).astype(BF16)
            dv.append(mm(prob.astype(BF16), g2))
            dk.append(mm(sgrad, q2))
            dq.append(mm(k_t[h * HD : (h + 1) * HD], sgrad))
        proj[:, lanes] = (jnp.concatenate(dq, axis=0) * (HD ** -0.5)).astype(BF16).T
        proj[:, k_lanes] = jnp.where(low_half, dk[0], dk[1]).astype(BF16)
        proj[:, v_lanes] = jnp.where(low_half, dv[0], dv[1]).astype(BF16)
    gvec[4:5, :] += col_sum(proj[:, :d].astype(F32))
    gvec[5:6, :] += col_sum(proj[:, 2 * d :].astype(F32))


def attn_bwd(first, last, dh, qkv, segc, segr, wout, gvec, before):
    tokens, d = dh.shape
    row = lambda width: pl.BlockSpec((ROW, width), lambda i: (i + first, 0))
    shapes = [jax.ShapeDtypeStruct((tokens, 3 * d), BF16), jax.ShapeDtypeStruct((tokens, d), BF16)]
    if before is None:
        kernel = lambda *refs: attn_bwd_kernel(first, *refs[:6], None, None, *refs[6:])
    else:
        kernel = lambda *refs: attn_bwd_kernel(first, *refs)
    return pl.pallas_call(
        kernel,
        grid=(last - first,),
        in_specs=[row(d), row(3 * d), whole(wout.shape), pl.BlockSpec((1, ROW, 2), lambda i: (i + first, 0, 0)),
                  pl.BlockSpec((1, 2, ROW), lambda i: (i + first, 0, 0)), whole(gvec.shape)]
        + ([] if before is None else [ANY, ANY]),
        out_specs=[row(3 * d), row(d), whole(gvec.shape)],
        out_shape=shapes + [jax.ShapeDtypeStruct(gvec.shape, F32)],
        input_output_aliases={} if before is None else {6: 0, 7: 1},
        compiler_params=pltpu.CompilerParams(vmem_limit_bytes=60 * MIB),
        cost_estimate=BRIEF,
        name="attn_bwd",
    )(dh, qkv, wout, segc, segr, gvec, *(before or ()))


def attn_grad_kernel(dims, goals, here_ref, x_ref, att_ref, proj_ref, branch_ref, gvec, gbup, *refs):
    total = goals[0][0].count
    grads, (x_t, wide, out, main, extra, sems) = refs[:total], refs[total:]
    npb, npa, r, wq, wo, rows_per, w1, w2 = dims
    step = pl.program_id(0)
    d = x_ref.shape[1]
    c = wq + wo

    def widen(piece):
        if piece.shape[1] == c:
            return piece
        return jnp.concatenate([piece, jnp.zeros((piece.shape[0], c - piece.shape[1]), F32)], axis=1)

    def multiply(g):
        wide[:, g * d : (g + 1) * d] = mm(x_t[...], proj_ref[...]).astype(BF16)

    def fill(g):
        for a in range(npa):
            if -(-(a + 1) * wq // d) == g:
                main[a] = jnp.concatenate([wide[:, a * wq : (a + 1) * wq], out[:, a * wo : (a + 1) * wo]], axis=1)

    @pl.when(step == 0)
    def _():
        x_t[...] = x_ref[...].T
        multiply(0)
        out[...] = mm(att_ref[...].T, branch_ref[...]).astype(BF16)

    for g in range(1, 3):
        @pl.when(step == g)
        def _():
            multiply(g)
            fill(g)

    @pl.when(step == 3)
    def _():
        fill(3)
        for b in range(npb):
            for a in range(npa):
                rows = [widen(gvec[b * rows_per : (b + 1) * rows_per, a * w1 : (a + 1) * w1]),
                        widen(gbup[b : b + 1, a * w2 : (a + 1) * w2]),
                        jnp.zeros((EXTRA - 1 - rows_per, c), F32)]
                extra[b * npa + a] = jnp.concatenate(rows, axis=0).astype(BF16)
        for goal, low, high in goals:
            top = min(high, r)
            for index, lead, b, a in goal.blocks(here_ref):
                target = grads[index]
                start = b * r + low
                if not isinstance(start, int):
                    start = pl.multiple_of(start, 16)
                pltpu.make_async_copy(main.at[a, pl.ds(start, top - low)], target.at[lead + (pl.ds(low, top - low),)],
                                      sems.at[0]).start()
                if high > r:
                    pltpu.make_async_copy(extra.at[b * npa + a], target.at[lead + (pl.ds(r, EXTRA),)], sems.at[1]).start()
        pltpu.make_async_copy(main, main, sems.at[0]).wait()
        pltpu.make_async_copy(extra, extra, sems.at[1]).wait()


def attn_grad(dims, goals, here, x, att, proj, branch, gvec, gbup):
    npb, npa, r, wq, wo, rows_per, w1, w2 = dims
    tokens, d = x.shape
    c = wq + wo
    return pl.pallas_call(
        functools.partial(attn_grad_kernel, dims, goals),
        grid=(4,),
        in_specs=[SMEM, whole(x.shape), whole(att.shape), pl.BlockSpec((tokens, d), lambda i: (0, jnp.minimum(i, 2))),
                  whole(branch.shape), whole(gvec.shape), whole(gbup.shape)],
        out_specs=[ANY] * goals[0][0].count,
        out_shape=[jax.ShapeDtypeStruct(goals[0][0].lead + (goals[-1][2], c), BF16)] * goals[0][0].count,
        scratch_shapes=[pltpu.VMEM((d, tokens), BF16), pltpu.VMEM((d, 3 * d), BF16), pltpu.VMEM((d, d), BF16),
                        pltpu.VMEM((npa, d, c), BF16),
                        pltpu.VMEM((npb * npa, EXTRA, c), BF16), pltpu.SemaphoreType.DMA((2,))],
        compiler_params=pltpu.CompilerParams(vmem_limit_bytes=60 * MIB),
        cost_estimate=BRIEF,
        name="attn_grad",
    )(here, x, att, proj, branch, gvec, gbup)


def input_grad_kernel(proj_ref, weight_ref, dh_ref, out_ref):
    out_ref[...] = mm_nt(proj_ref[...], weight_ref[...]) + dh_ref[...]


def input_grad(proj, wqkv, dh):
    tokens, d = dh.shape
    row = lambda width: pl.BlockSpec((ROW, width), lambda i: (i, 0))
    return pl.pallas_call(
        input_grad_kernel,
        grid=(tokens // ROW,),
        in_specs=[row(3 * d), whole(wqkv.shape), row(d)],
        out_specs=row(d),
        out_shape=jax.ShapeDtypeStruct((tokens, d), F32),
        compiler_params=pltpu.CompilerParams(vmem_limit_bytes=60 * MIB),
        cost_estimate=BRIEF,
        name="input_grad",
    )(proj, wqkv, dh)


class Blocks:
    def __init__(self, npb, npa, d, ff):
        self.npb, self.npa, self.d, self.ff = npb, npa, d, ff
        self.r, self.wq, self.wo, self.c = d // npb, 3 * d // npa, d // npa, ff // npa
        self.dr, self.dc = d // npa, ff // npb
        self.rows_per, self.w1, self.w2 = 8 // npb, d // npa, ff // (npa * npb)
        self.direct = self.c % 128 == 0 and self.r % 16 == 0 and self.dr % 16 == 0
        if self.direct:
            self.dims = (npb, npa, self.r, self.wq, self.wo, self.rows_per, self.w1, self.w2)
        else:
            self.dims = (1, 1, d, 3 * d, d, 8, d, ff)

    def pack(self, w_qkv, w_out, w_up, w_down, norm_bias, bias_up):
        c = self.wq + self.wo
        vec = jnp.pad(norm_bias, ((0, 0), (0, 0), (0, c - self.w1)))
        bup = jnp.pad(bias_up[:, None, :], ((0, 0), (0, EXTRA - 1 - self.rows_per), (0, c - self.w2)))
        attn = jnp.concatenate([jnp.concatenate([w_qkv, w_out], axis=2), vec, bup], axis=1)
        down_t = jnp.swapaxes(w_down, 1, 2)
        down = jnp.concatenate([down_t[:, :, j : j + self.c] for j in range(0, self.dc, self.c)], axis=1)
        return attn, jnp.concatenate([w_up, down], axis=1)

    def from_blocks(self, attn, ffn):
        if self.direct:
            return attn, ffn
        d, ff, r = self.d, self.ff, self.r
        rows = lambda part, height: part.transpose(0, 2, 1, 3).reshape(height, -1)
        qkv = rows(attn[:, :, :r, : self.wq], d)
        out = rows(attn[:, :, :r, self.wq :], d)
        vec = rows(attn[:, :, r : r + self.rows_per, : self.w1], 8)
        bup = attn[:, :, r + self.rows_per, : self.w2].reshape(1, ff)
        vec = jnp.pad(vec, ((0, 0), (0, 3 * d)))
        bup = jnp.pad(bup, ((0, EXTRA - 9), (0, 4 * d - ff)))
        wide = jnp.concatenate([jnp.concatenate([qkv, out], axis=1), vec, bup], axis=0)
        up = rows(ffn[:, :, :r], d)
        pieces = self.dc // self.c
        down = ffn[:, :, r:].reshape(self.npb, self.npa, pieces, self.dr, self.c)
        down = down.transpose(1, 3, 0, 2, 4).reshape(d, ff)
        return wide[None, None], jnp.concatenate([up, down])[None, None]

    def to_blocks(self, attn, ffn):
        if self.direct:
            return attn, ffn
        d, ff, npb, npa = self.d, self.ff, self.npb, self.npa
        blocks = lambda part, height: part.reshape(npb, height, npa, -1).transpose(0, 2, 1, 3)
        wide = attn[0, 0]
        c = self.wq + self.wo
        main = jnp.concatenate([blocks(wide[:d, : 3 * d], self.r), blocks(wide[:d, 3 * d :], self.r)], axis=3)
        vec = blocks(wide[d : d + 8, :d], self.rows_per)
        vec = jnp.pad(vec, ((0, 0), (0, 0), (0, 0), (0, c - self.w1)))
        bup = wide[d + 8, :ff].reshape(npb, npa, 1, self.w2)
        bup = jnp.pad(bup, ((0, 0), (0, 0), (0, EXTRA - 1 - self.rows_per), (0, c - self.w2)))
        pieces = self.dc // self.c
        down = ffn[0, 0, d:].reshape(npa, self.dr, npb, pieces, self.c).transpose(2, 0, 3, 1, 4)
        down = down.reshape(npb, npa, pieces * self.dr, self.c)
        return jnp.concatenate([main, vec, bup], axis=2), jnp.concatenate([blocks(ffn[0, 0, :d], self.r), down], axis=2)

    def unpack(self, attn, ffn):
        r = self.r
        attn, ffn = jnp.stack(attn), jnp.stack(ffn)
        down = ffn[:, r:]
        down = jnp.concatenate([down[:, j * self.dr : (j + 1) * self.dr] for j in range(self.dc // self.c)], axis=2)
        return (attn[:, :r, : self.wq], attn[:, :r, self.wq :], ffn[:, :r], jnp.swapaxes(down, 1, 2),
                attn[:, r : r + self.rows_per, : self.w1], attn[:, r + self.rows_per, : self.w2])


BOTH = ("pb", "pa")
BITS = {"core": 8, "y": 16, "z1": 2, "z2": 4, "z3": 6, "x": 1, "xy": 17}


def swap(block, way):
    return lax.ppermute(block, BOTH, [(i, i ^ BITS[way]) for i in range(32)])


class Gather:
    def __init__(self, block, ways):
        self.held, self.ways = [block], ways

    def after(self, *others):
        late = [held for other in others for held in other.held]
        self.held = list(lax.optimization_barrier((tuple(self.held), tuple(late)))[0])

    def step(self, stage):
        if stage == 0:
            block = self.held[0]
            self.held = [jnp.stack([block] + [swap(block, way) for way in ("z1", "z2", "z3")])]
        else:
            way = self.ways[stage - 1] if stage < 3 else "core"
            self.held = self.held + [swap(part, way) for part in self.held]


def gather_heads(block):
    near = jnp.stack([block] + [swap(block, way) for way in ("z1", "z2", "z3")])
    wide = jnp.stack([near] + [swap(near, way) for way in ("x", "y", "xy")])
    wide = wide.reshape((-1,) + block.shape)
    return [wide, swap(wide, "core")]


HEAD_ORDER = [c ^ s ^ z for c in (0, 8) for s in (0, 1, 16, 17) for z in (0, 2, 4, 6)]


def cut_out(array, pick, rows):
    depth = len(pick)
    low = list(pick) + [0] * (array.ndim - depth)
    high = [index + 1 for index in pick] + list(array.shape[depth:])
    low[-2], high[-2] = rows.start, rows.stop
    return lax.slice(array, low, high).reshape([h - l for l, h in zip(low, high)][depth:])


class Scatter:
    def __init__(self, keep, send, cut):
        self.shared = [keep, send]
        self.own = [[], []]
        self.rows = [slice(0, cut), slice(cut, keep.shape[-2])]
        self.spot = ()

    def sum(self, part, j=None):
        pick = self.spot if j is None else self.spot + (j,)
        terms = [cut_out(array, pick, self.rows[part]) for array in self.shared]
        for age, array in self.own[part]:
            terms.append(cut_out(array, pick[age:], slice(0, array.shape[-2])))
        return sum(term.astype(F32) for term in terms)

    def step(self, stage, line):
        if stage == 0:
            self.shared = [self.shared[0], swap(line.wait((self.shared[1],))[0], "core")]
            return
        self.fresh(line)
        if stage < 3:
            parts = [self.sum(part, 1).astype(BF16) for part in range(2)]
            line.mark(parts)
            self.spot += (0,)
            for part, ways in enumerate((("y", "x"), ("x", "y"))):
                self.own[part].append((len(self.spot), swap(parts[part], ways[stage - 1])))
            return
        parts = [jnp.concatenate([self.sum(part, j) for part in range(2)]).astype(BF16) for j in range(1, 4)]
        line.mark(parts)
        self.spot += (0,)
        self.last = [swap(part, f"z{j + 1}") for j, part in enumerate(parts)]

    def fresh(self, line):
        if self.spot:
            arrays = line.wait(tuple(own[-1][1] for own in self.own))
            for own, array in zip(self.own, arrays):
                own[-1] = (own[-1][0], array)
        else:
            self.shared[1] = line.wait((self.shared[1],))[0]

    def total(self, line):
        last = line.wait(tuple(self.last))
        kept = jnp.concatenate([self.sum(part) for part in range(2)])
        return line.mark(kept + sum(term.astype(F32) for term in last))


class Line:
    def __init__(self):
        self.last = None

    def wait(self, operands):
        if self.last is None:
            return operands
        return lax.optimization_barrier((operands, self.last))[0]

    def mark(self, result):
        self.last = jax.tree.leaves(result)[0]
        return result

    def run(self, step, *operands):
        return self.mark(step(*self.wait(operands)))


def body(questions, passages, cot_questions, cot_passages, question_lengths, segment_lengths, positives, w_qkv, w_out, w_up,
         w_down, norm_bias, bias_up):
    q_count, q_len, d = questions.shape
    row_count, row_len, _ = passages.shape
    segs = segment_lengths.shape[1]
    npb, npa = lax.axis_size("pb"), lax.axis_size("pa")
    size = Blocks(npb, npa, d, bias_up.shape[1] * npb * npa)
    dims = size.dims
    near = size.direct and (npb, npa) == (4, 8)
    pb, pa = lax.axis_index("pb"), lax.axis_index("pa")
    device = pb * npa + pa
    here = jnp.stack([pb // 2, pb % 2, pa // 2, pa % 2]).astype(jnp.int32)
    order = (("y", "x"), ("x", "y"))

    attn_pack, ffn_pack = size.pack(w_qkv, w_out, w_up, w_down, norm_bias, bias_up)
    mesh_order = Place(dims[0], dims[1], None, False)
    one_array = FfnPlace(mesh_order)
    if near:
        ffn_all = lax.all_gather(ffn_pack, BOTH, axis=0).reshape((npb, npa) + ffn_pack.shape)
        parts = [Gather(attn_pack[e], order[e]) for e in range(2)]
        for stage in range(4):
            for each in parts:
                each.step(stage)
        attn_w = [each.held for each in parts]
        attn_into = [Place(npb, npa, order[e][0], True) for e in range(2)]
        ffn_w = [[ffn_all]] * 2
        ffn_into = [FfnPlace(mesh_order, e=e) for e in range(2)]
    else:
        attn_all = lax.all_gather(attn_pack, BOTH, axis=0).reshape((npb, npa) + attn_pack.shape)
        ffn_all = lax.all_gather(ffn_pack, BOTH, axis=0).reshape((npb, npa) + ffn_pack.shape)
        attn_w, ffn_w = zip(*[size.from_blocks(attn_all[:, :, e], ffn_all[:, :, e]) for e in range(2)])
        attn_w = [[blocks] for blocks in attn_w]
        ffn_w = [[blocks] for blocks in ffn_w]
        attn_into = [mesh_order] * 2
        ffn_into = [one_array] * 2

    per_row = ROW // q_len
    q_rows = q_count // per_row
    token = jnp.arange(ROW, dtype=jnp.int32)
    q_seg = jnp.broadcast_to(token // q_len, (q_rows, ROW))
    q_valid = (token % q_len)[None, :] < jnp.repeat(question_lengths.reshape(q_rows, per_row), q_len, axis=1)
    starts = jnp.cumsum(segment_lengths, axis=1) - segment_lengths
    p_seg = jnp.sum((token[None, None, :] >= starts[:, :, None]).astype(jnp.int32), axis=1)
    segr = (jnp.stack([q_seg, jnp.where(q_valid, q_seg, -1)], axis=1), jnp.stack([p_seg, p_seg], axis=1))
    segc = tuple(jnp.swapaxes(pair, 1, 2) for pair in segr)
    spots = (jnp.broadcast_to(jnp.arange(per_row, dtype=jnp.int32) * q_len, (q_rows, per_row)), starts)
    xs = (questions.reshape(-1, d), passages.reshape(-1, d))
    cots = [cot_questions.reshape(-1, d), cot_passages.reshape(-1, d)]
    p_count = row_count * segs

    def by_step(spots):
        rows = FFN_ROW // ROW
        base = jnp.arange(spots.shape[0], dtype=jnp.int32) % rows * ROW
        return (spots + base[:, None]).reshape(-1, rows * spots.shape[1])

    spots = tuple(by_step(each) for each in spots)
    own_hits = lax.dynamic_slice_in_dim(positives, pa * q_count, q_count)
    code = jnp.pad(jnp.stack([own_hits // 256, own_hits % 256], axis=1).astype(BF16), ((0, 0), (0, d - 2)))
    listed = device ^ jnp.array(HEAD_ORDER, jnp.int32) if near else jnp.arange(npb * npa, dtype=jnp.int32)
    ids = (listed[:, None] * p_count + jnp.arange(p_count, dtype=jnp.int32)[None, :]).reshape(1, -1)
    own_ids = device * p_count + jnp.arange(p_count, dtype=jnp.int32)[None, :]

    line = Line()
    half = [
        line.run(lambda x, *packs, e=e: attn_fwd(dims, attn_into[e], here, packs, x, segc[e], segr[e]), xs[e], *attn_w[e])
        for e in range(2)
    ]
    done = [None, None]
    for e in (0, 1):
        done[e] = line.run(
            lambda *packs, e=e: ffn_fwd(ffn_into[e], here, spots[e], packs, half[e][2], half[e][6], half[e][7]), *ffn_w[e])
    own = jnp.concatenate([done[1][5].reshape(p_count, d).astype(BF16), done[0][5].reshape(q_count, d).astype(BF16), code])
    heads = gather_heads(own) if near else [lax.all_gather(own, BOTH, axis=0)]
    losses, *gcls = loss_part(ids, own_ids, heads, own[None], spots[0].shape, spots[1].shape)

    def ffn_step(e, goal, cot):
        _, _, xhat, inv1, _, _, vec, bup = half[e]
        act, slope, norm2, inv2, _, _ = done[e]
        dh, *blocks, gvec, gbup = ffn_bwd(ffn_into[e], goal, here, spots[e], ffn_w[e], cot, gcls[e], norm2,
                                          inv2, act, slope, xhat, inv1, vec, bup.shape)
        return dh, blocks, gvec, gbup

    def attn_rows(e, first, last, dh, gvec, before):
        return attn_bwd(first, last, dh, half[e][0], segc[e], segr[e], half[e][5], gvec, before)

    def attn_weights(e, goals, rows, gbup):
        return attn_grad(dims, goals, here, xs[e], half[e][1], rows[0], rows[1], rows[2], gbup)

    def scatter(blocks, dtype=F32):
        flat = blocks.reshape((npb * npa,) + blocks.shape[2:])
        return lax.psum_scatter(flat, BOTH, scatter_dimension=0, tiled=False).astype(dtype)

    counts = (q_rows, row_count)
    if near:
        whole_block = attn_pack.shape[1]
        cut = whole_block // 32 * 16 + 16
        y_first, x_first = (Place(npb, npa, way[0], False) for way in order)
        goals = [(y_first, 0, cut), (x_first, cut, whole_block)]
        line = Line()
        dh_q, blocks_q, gvec_q, gbup_q = line.run(lambda cot: ffn_step(0, one_array, cot), cots[0])
        sum_q = scatter(blocks_q[0], BF16)
        dh_p, blocks_p, gvec_p, gbup_p = line.run(lambda cot: ffn_step(1, FfnPlace(y_first, x_first), cot), cots[1])
        ffn_p = Scatter(*blocks_p, size.r)
        ffn_p.step(0, line)
        rows_q = line.run(lambda dh: attn_rows(0, 0, q_rows, dh, gvec_q, None), dh_q)
        ffn_p.step(1, line)
        attn_q = Scatter(*line.run(lambda *rows: attn_weights(0, goals, rows, gbup_q), *rows_q), cut)
        middle = row_count // 2
        rows_p = line.run(lambda dh: attn_rows(1, 0, middle, dh, gvec_p, None), dh_p)
        ffn_p.step(2, line)
        attn_q.step(0, line)
        rows_p = line.run(lambda *rows: attn_rows(1, middle, row_count, dh_p, rows[2], rows[:2]), *rows_p)
        ffn_p.step(3, line)
        attn_q.step(1, line)
        attn_p = Scatter(*line.run(lambda *rows: attn_weights(1, goals, rows, gbup_p), *rows_p), cut)
        attn_q.step(2, line)
        sums = [ffn_p.total(line)]
        attn_p.step(0, line)
        gx_q = line.run(lambda proj: input_grad(proj, half[0][4], dh_q), rows_q[0])
        attn_p.step(1, line)
        attn_q.step(3, line)
        gx_p = line.run(lambda proj: input_grad(proj, half[1][4], dh_p), rows_p[0])
        gx = (gx_q, gx_p)
        attn_p.step(2, line)
        sums.append(attn_q.total(line))
        attn_p.step(3, line)
        sum_q = line.wait((sum_q,))[0]
        sums.append(attn_p.total(line))
        ffn_sum = [sum_q.astype(F32), sums[0]]
        attn_sum = sums[1:]
    else:
        pairs, gx = [], []
        for e in range(2):
            dh, blocks, gvec, gbup = ffn_step(e, one_array, cots[e])
            rows = attn_rows(e, 0, counts[e], dh, gvec, None)
            got = attn_weights(e, [(mesh_order, 0, dims[2] + EXTRA)], rows, gbup)
            pairs.append(size.to_blocks(got[0], blocks[0]))
            gx.append(input_grad(rows[0], half[e][4], dh))
        attn_sum = [scatter(pair[0]) for pair in pairs]
        ffn_sum = [scatter(pair[1]) for pair in pairs]
    outs = size.unpack(attn_sum, ffn_sum)
    return (
        done[0][4].reshape(questions.shape),
        done[1][4].reshape(passages.shape),
        losses[:, 0],
        gx[0].reshape(questions.shape),
        gx[1].reshape(passages.shape),
    ) + outs


def solution(mesh):
    rows = P(BOTH, None, None)
    shard = P(None, "pb", "pa")
    vector = P(None, BOTH)
    in_specs = (rows, rows, rows, rows, P(BOTH), P(BOTH, None), P("pb"), shard, shard, shard, shard, shard, vector)
    out_specs = (rows, rows, P(BOTH), rows, rows, shard, shard, shard, shard, shard, vector)
    return jax.shard_map(body, mesh=mesh, in_specs=in_specs, out_specs=out_specs, check_vma=False)
```
